256 devices in a mesh: tm: 32 (over x, z_lo, core), space: 8 (over y, z_hi).
Axes of the slice: x: 4, y: 4, z: 8 (z_hi: 2, z_lo: 4; z = z_hi * 4 + z_lo), core: 2. Of those that a mesh axis runs over, the one named last changes fastest.
Arguments:
- initial: float32 [64, 64, 128], P('space'), may hold values from -6 to 6
- forcing: bfloat16 [128, 64, 64, 128], P('tm', 'space'), may hold values from -4 to 4
- brick_blocks: bfloat16 [64, 64, 448], P('space'), may hold values from -1 to 1
- neighbours: int32 [64, 6], P('space'), may hold values from 0 to 63, as said below
- coarse_modes: float32 [8, 64], replicated, may hold values from -0.75 to 0.75
- coarse_blocks: float32 [64, 8, 8], P('space'), may hold values from -1 to 1.2
Outputs:
- solution: float32 [128, 64, 64, 128], P('tm', 'space')
- last_defect: float32 [32, 64, 64, 128], P('tm', 'space')
The draws below stay inside these ranges and needn't reach their ends.
Inputs may be any that keep to these rules, and one draw needn't show every extreme that they name: `neighbours`: each brick's 6 slots name distinct bricks other than itself, in a random slot order, each at most 4 positions away along the periodic brick order; every brick names the bricks directly before and after it and one brick exactly 4 away.
All inputs are finite; a program needn't handle non-finite values.
Results may differ from the reference program's by a relative error of at most 0.014.
Values may be sent and summed in bfloat16 or wider, within the bound.
A program may use at most 64 MiB of HBM per device.

```python
import jax
import jax.numpy as jnp
from jax import lax

BRICK = 64
ENS = 128
NB = 6
REACH = 4
Q = 8
SWEEPS = 3
STEPS = 4
ITERS = 2
BRICKS = 64
NT = 128
N_TM = 32


def draw_brick_blocks(key, part):
    first_key = jax.random.fold_in(jax.random.fold_in(key, 11), 0)
    block_shape = (BRICKS, BRICK, (NB + 1) * BRICK)
    random_part = jnp.clip(jax.random.normal(first_key, block_shape, jnp.float32), -6.0, 6.0)
    spread = jnp.ones((BRICKS, 1, 1), jnp.float32)
    row_ids = jnp.arange(BRICK)[:, None]
    col_ids = jnp.arange((NB + 1) * BRICK)[None, :]
    leading = col_ids < BRICK
    entry_scale = jnp.where(leading, 0.25, 0.15 * spread) / jnp.sqrt(jnp.float32(BRICK))
    identity = (row_ids == col_ids).astype(jnp.float32)
    return (0.7 * identity + entry_scale * random_part).astype(jnp.bfloat16)


def draw_neighbours(key, part):
    sign_key, pick_key, order_key = jax.random.split(jax.random.fold_in(key, 37), 3)
    direction = 2 * jax.random.randint(sign_key, (BRICKS, 1), 0, 2) - 1
    middle = jnp.arange(2, REACH, dtype=jnp.int32)
    both_sides = jnp.concatenate([middle, -middle])[None, :]
    candidates = jnp.concatenate([jnp.broadcast_to(both_sides, (BRICKS, 2 * REACH - 4)), -direction * REACH], 1)
    pool_size = 2 * REACH - 3
    scores = jax.random.randint(pick_key, (BRICKS, pool_size), 0, 1 << 20) * pool_size + jnp.arange(pool_size, dtype=jnp.int32)
    chosen = jnp.take_along_axis(candidates, jnp.argsort(scores, axis=1)[:, :NB - 3], 1)
    fixed_part = jnp.concatenate([-jnp.ones((BRICKS, 1), jnp.int32), jnp.ones((BRICKS, 1), jnp.int32), direction * REACH], 1)
    offsets = jnp.concatenate([fixed_part, chosen], 1)
    order_scores = jax.random.randint(order_key, (BRICKS, NB), 0, 1 << 20) * NB + jnp.arange(NB, dtype=jnp.int32)
    offsets = jnp.take_along_axis(offsets, jnp.argsort(order_scores, axis=1), 1)
    return jnp.mod(jnp.arange(BRICKS, dtype=jnp.int32)[:, None] + offsets, BRICKS).astype(jnp.int32)


def draw_coarse_blocks(key, part):
    first_key, second_key = jax.random.split(jax.random.fold_in(key, 23))
    chain_length = NT // STEPS
    horizon = jnp.exp(jax.random.uniform(first_key, (BRICKS, Q), jnp.float32, jnp.log(0.25), jnp.log(8.0)))
    random_part = jnp.clip(jax.random.normal(second_key, (BRICKS, Q, Q), jnp.float32), -3.0, 3.0)
    decay_rates = jnp.power(0.1, horizon / chain_length)
    identity = jnp.eye(Q, dtype=jnp.float32)
    return decay_rates[:, :, None] * identity + 0.1 / jnp.sqrt(jnp.float32(Q)) * random_part


def block_scale(own_key, dims, cuts, low, high):
    def one(position, blocks):
        heights = jax.random.uniform(jax.random.fold_in(jax.random.fold_in(own_key, 6), position), (blocks,), jnp.float32, low / len(cuts), high / len(cuts))
        return jnp.repeat(jnp.exp(heights), dims[position] // blocks).reshape((-1,) + (1,) * (len(dims) - position - 1))

    level = one(*cuts[0])
    for cut in cuts[1:]:
        level = level * one(*cut)
    return level


def scatter_about(own_key, shape, scale, bound, cuts=(), held_as=jnp.bfloat16):
    gain = block_scale(own_key, shape, cuts, -0.22, 0.18) if cuts else 1.0
    array = jax.random.normal(own_key, shape, jnp.float32) * scale * gain
    return jnp.minimum(jnp.maximum(array, -bound), bound).astype(held_as)


def setup_inputs(seed: int = 0) -> dict:
    keys = jax.random.split(jax.random.key(seed), 7)
    initial = scatter_about(keys[0], (BRICKS, BRICK, ENS), 1.0, 6.0, ((0, 8),), jnp.float32)
    forcing = scatter_about(keys[1], (NT, BRICKS, BRICK, ENS), 0.5, 4.0, ((0, 32), (1, 8)))
    brick_blocks = draw_brick_blocks(jax.random.fold_in(keys[6], 71), 0)
    neighbours = draw_neighbours(jax.random.fold_in(keys[6], 71), 0)
    coarse_modes = scatter_about(keys[4], (Q, BRICK), BRICK ** -0.5, 0.75, (), jnp.float32)
    coarse_blocks = draw_coarse_blocks(jax.random.fold_in(keys[6], 71), 0)
    return {"initial": initial, "forcing": forcing, "brick_blocks": brick_blocks, "neighbours": neighbours, "coarse_modes": coarse_modes, "coarse_blocks": coarse_blocks}


highest = lax.Precision.HIGHEST


def rounded(values):
    return lax.optimization_barrier(values.astype(jnp.bfloat16)).astype(jnp.float32)


def propagate(values, diagonal, off_parts, neighbours):
    iterate = jnp.einsum("bij,sbje->sbie", diagonal, rounded(values))
    for sweep_index in range(SWEEPS - 1):
        source = rounded(iterate)
        coupled = jnp.zeros_like(values)
        for column in range(NB):
            coupled = coupled + jnp.einsum("bij,sbje->sbie", off_parts[column], source[:, neighbours[:, column]])
        iterate = jnp.einsum("bij,sbje->sbie", diagonal, rounded(values - coupled))
    return iterate


def reference(initial, forcing, brick_blocks, neighbours, coarse_modes, coarse_blocks):
    blocks = brick_blocks.astype(jnp.float32)
    diagonal = blocks[:, :, :BRICK]
    off_parts = [blocks[:, :, BRICK * (column + 1):BRICK * (column + 2)] for column in range(NB)]
    forcing_steps = forcing.reshape(N_TM, STEPS, BRICKS, BRICK, ENS)
    slice_ends = jnp.zeros((N_TM, BRICKS, BRICK, ENS), jnp.float32)
    slice_starts = jnp.concatenate([initial[None], slice_ends[:-1]], 0)

    def coarse_step(carried, new_term):
        follow = jnp.einsum("bpq,bqe->bpe", coarse_blocks, carried, precision=highest) + new_term
        return follow, follow

    defect = slice_ends
    for count_iter in range(ITERS):
        current = slice_starts
        for substep in range(STEPS - 1):
            current = propagate(current, diagonal, off_parts, neighbours) + forcing_steps[:, substep].astype(jnp.float32)
        defect = propagate(current, diagonal, off_parts, neighbours) + forcing_steps[:, STEPS - 1].astype(jnp.float32) - slice_ends
        restricted = jnp.einsum("qc,sbce->sbqe", coarse_modes, defect, precision=highest)
        start_error = jnp.zeros((BRICKS, Q, ENS), jnp.float32)
        final_error, errors = lax.scan(coarse_step, start_error, restricted)
        slice_ends = slice_ends + jnp.einsum("qc,sbqe->sbce", coarse_modes, errors, precision=highest)
        slice_starts = jnp.concatenate([initial[None], slice_ends[:-1]], 0)
    outputs = []
    current = slice_starts
    for substep in range(STEPS - 1):
        current = propagate(current, diagonal, off_parts, neighbours) + forcing_steps[:, substep].astype(jnp.float32)
        outputs.append(current)
    outputs.append(slice_ends)
    solution = jnp.stack(outputs, 1).reshape(NT, BRICKS, BRICK, ENS)
    return solution, defect
```

```python
import functools

import jax
import jax.numpy as jnp
from jax import lax
from jax.experimental import pallas as pl
from jax.experimental.pallas import tpu as pltpu
from jax.sharding import PartitionSpec as P

BRICK = 64
ENS = 128
NB = 6
REACH = 4
Q = 8
STEPS = 4
ITERS = 2
HERE = 8
SLICES = 32
ROWS = HERE * BRICK
HALF = ROWS // 2

MESH = pl.DeviceIdType.MESH
HIGHEST = lax.Precision.HIGHEST
F32 = jnp.float32
BF16 = jnp.bfloat16


def dot(a, b):
    return jnp.dot(a, b, preferred_element_type=F32)


def dot32(a, b):
    return jnp.dot(a, b, preferred_element_type=F32, precision=HIGHEST)


def kernel(
    init_ref, forcing_ref, blocks_ref, neighbours_ref, modes_ref, coarse_ref,
    sol_ref, def_ref,
    fields, weights, home_nbr, nbr, start, state, band, diag, ext0, ext1,
    restrict, toep, strip, r_buf, in0, in1, e_buf, got0, got1, e_prev, e_here, ends, stage,
    field_sem, weight_sem, nbr_sem, start_sem, halo_send, halo_recv,
    swap_send, sc_send, sc_recv, out_send, sol_recv, def_recv,
):
    tm = lax.axis_index("tm")
    sp = lax.axis_index("space")
    c = lax.rem(tm, 2)
    zl = lax.rem(tm // 2, 4)
    x = tm // 8
    y = sp // 2
    zh = lax.rem(sp, 2)
    keeps = c == zh
    moves = c != zh
    j = x * 8 + zl * 2 + zh
    q = 2 * y + c
    partner = (tm - c + zh, sp - zh + c)
    q_low = lax.rem(q + 7, 8)
    q_high = lax.rem(q + 1, 8)
    low = (tm - c + lax.rem(q_low, 2), (q_low // 2) * 2 + zh)
    high = (tm - c + lax.rem(q_high, 2), (q_high // 2) * 2 + zh)

    def worker(slice_id):
        return (
            (slice_id // 8) * 8 + lax.rem(slice_id // 2, 4) * 2 + c,
            2 * y + lax.rem(slice_id, 2),
        )

    barrier = pltpu.get_barrier_semaphore()
    pl.semaphore_signal(barrier, inc=1, device_id=low, device_id_type=MESH)
    pl.semaphore_signal(barrier, inc=1, device_id=high, device_id_type=MESH)

    @pl.when(moves)
    def _():
        pl.semaphore_signal(barrier, inc=1, device_id=partner, device_id_type=MESH)

    @pl.loop(1, SLICES)
    def _(d):
        pl.semaphore_signal(
            barrier, inc=1, device_id=worker(lax.rem(j + d, SLICES)), device_id_type=MESH
        )

    home_nbr[...] = jnp.zeros_like(home_nbr)
    home_nbr[:, 0:NB] = neighbours_ref[...]
    pl.semaphore_wait(barrier, jnp.where(moves, SLICES + 2, SLICES + 1))

    def remote(src, dst, send, recv, device):
        return pltpu.make_async_remote_copy(
            src_ref=src, dst_ref=dst, send_sem=send, recv_sem=recv,
            device_id=device, device_id_type=MESH,
        )

    def arrived(ref, sem):
        pltpu.make_async_copy(ref, ref, sem).wait()

    @pl.when(keeps)
    def _():
        pltpu.make_async_copy(blocks_ref, weights, weight_sem).start()
        for i in range(STEPS):
            pltpu.make_async_copy(forcing_ref.at[i], fields.at[i], field_sem.at[i]).start()
        pltpu.make_async_copy(home_nbr, nbr, nbr_sem).start()

    @pl.when(moves)
    def _():
        remote(home_nbr, nbr, swap_send.at[5], nbr_sem, partner).start()
        remote(blocks_ref, weights, swap_send.at[4], weight_sem, partner).start()
        for i in range(STEPS):
            remote(
                forcing_ref.at[i], fields.at[i], swap_send.at[i], field_sem.at[i], partner
            ).start()

    @pl.when((tm == 0) & (zh == 1))
    def _():
        remote(init_ref, start, swap_send.at[6], start_sem, partner).start()

    @pl.when((tm == 0) & (zh == 0))
    def _():
        pltpu.make_async_copy(init_ref, start, start_sem).start()

    modes = modes_ref[...]
    wide = jnp.concatenate([jnp.concatenate([modes] * 4, axis=1)] * 4, axis=0)
    row = lax.broadcasted_iota(jnp.int32, (4 * Q, HALF), 0)
    col = lax.broadcasted_iota(jnp.int32, (4 * Q, HALF), 1)
    restrict[...] = jnp.where(row // Q == col // BRICK, wide, 0.0)

    own_brick = lax.rem(x, 2) * 4 + zl
    half = x // 2
    one = coarse_ref[own_brick]
    eye = (
        lax.broadcasted_iota(jnp.int32, (Q, Q), 0) == lax.broadcasted_iota(jnp.int32, (Q, Q), 1)
    ).astype(F32)
    powers = eye
    power = one
    while powers.shape[1] < SLICES * Q:
        powers = jnp.concatenate([dot32(power, powers), powers], axis=1)
        power = dot32(power, power)
    strip[:, 0 : SLICES * Q] = powers
    strip[:, SLICES * Q :] = jnp.zeros((Q, SLICES * Q), F32)
    both = strip[...]
    for i in range(SLICES):
        first = (SLICES - 1 - i) * Q
        toep[i * Q : (i + 1) * Q, :] = both[:, first : first + SLICES * Q]
    e_buf[0] = jnp.zeros((Q, ENS), F32)

    diag[...] = jnp.zeros_like(diag)
    band[...] = jnp.zeros_like(band)
    arrived(nbr, nbr_sem)
    arrived(weights, weight_sem)
    position = 8 * q + lax.broadcasted_iota(jnp.int32, (HERE, 128), 0)
    shift = lax.rem(nbr[...] - position + (REACH + 64), 64)
    for b in range(HERE):
        g, b4 = divmod(b, 4)
        rows = slice(b4 * BRICK, (b4 + 1) * BRICK)
        diag[g, rows, rows] = weights[b, :, 0:BRICK]
        offs = [weights[b, :, (k + 1) * BRICK : (k + 2) * BRICK].astype(F32) for k in range(NB)]
        where = [jnp.broadcast_to(shift[b : b + 1, k : k + 1], (BRICK, BRICK)) for k in range(NB)]
        for p in range(2 * REACH + 1):
            block = jnp.zeros((BRICK, BRICK), F32)
            for k in range(NB):
                block = jnp.where(where[k] == p, offs[k], block)
            first = (b4 + p) * BRICK
            band[g, rows, first : first + BRICK] = block.astype(BF16)

    def exchange(ext, values, slot):
        ext[HALF : 2 * HALF, :] = values(0).astype(BF16)
        down = remote(
            ext.at[pl.ds(HALF, HALF)], ext.at[pl.ds(3 * HALF, HALF)],
            halo_send.at[slot, 0], halo_recv.at[slot, 0], low,
        )
        down.start()
        ext[2 * HALF : 3 * HALF, :] = values(1).astype(BF16)
        up = remote(
            ext.at[pl.ds(2 * HALF, HALF)], ext.at[pl.ds(0, HALF)],
            halo_send.at[slot, 1], halo_recv.at[slot, 1], high,
        )
        up.start()
        near0 = dot(band[0, :, HALF:], ext[HALF : 3 * HALF, :])
        near1 = dot(band[1, :, : 2 * HALF], ext[HALF : 3 * HALF, :])
        down.wait_send()
        up.wait_send()
        down.wait_recv()
        up.wait_recv()
        return (
            near0 + dot(band[0, :, :HALF], ext[0:HALF, :]),
            near1 + dot(band[1, :, 2 * HALF :], ext[3 * HALF :, :]),
        )

    def propagate():
        values = [state[0:HALF, :], state[HALF:ROWS, :]]
        coupled = exchange(ext0, lambda g: dot(diag[g], values[g].astype(BF16)), 0)
        coupled = exchange(
            ext1, lambda g: dot(diag[g], (values[g] - coupled[g]).astype(BF16)), 1
        )
        return [dot(diag[g], (values[g] - coupled[g]).astype(BF16)) for g in range(2)]

    def halves(g):
        return slice(g * HALF, (g + 1) * HALF)

    def step(i):
        following = propagate()
        for g in range(2):
            state[halves(g), :] = following[g] + fields[i, halves(g), :].astype(F32)

    def deliver(n):
        target = sol_ref.at[n] if n < STEPS else def_ref

        @pl.when(keeps)
        def _():
            pltpu.make_async_copy(
                stage.at[n], target, sol_recv if n < STEPS else def_recv
            ).start()

        @pl.when(moves)
        def _():
            remote(
                stage.at[n], target, out_send.at[n], sol_recv if n < STEPS else def_recv, partner
            ).start()

    @pl.when(j == 0)
    def _():
        arrived(start, start_sem)
        state[...] = start[...]

    @pl.when(j != 0)
    def _():
        state[...] = jnp.zeros_like(state)

    ends[...] = jnp.zeros_like(ends)
    e_prev[...] = jnp.zeros_like(e_prev)
    e_here[...] = jnp.zeros_like(e_here)

    for it, (incoming, got) in enumerate(((in0, got0), (in1, got1))):

        @pl.loop(0, STEPS)
        def _(i):
            if it == 0:
                arrived(fields.at[i], field_sem.at[i])
            step(i)

        for g in range(2):
            defect = state[halves(g), :] - ends[halves(g), :]
            if it == ITERS - 1:
                stage[STEPS, halves(g), :] = defect.astype(BF16)
            r_buf[it, 4 * g : 4 * g + 4] = dot32(restrict[...], defect).reshape(4, Q, ENS)

        @pl.loop(0, 16)
        def _(w):
            brick = lax.rem(w, 8)
            owner_tm = ((w // 8) * 2 + brick // 4) * 8 + lax.rem(brick, 4) * 2 + c
            owner_sp = 2 * y + c
            mine = (owner_tm == tm) & (owner_sp == sp)

            @pl.when(mine)
            def _():
                incoming[j] = r_buf[it, brick]

            @pl.when(jnp.logical_not(mine))
            def _():
                remote(
                    r_buf.at[it, brick], incoming.at[j], sc_send.at[it, 0], sc_recv.at[it, 0],
                    (owner_tm, owner_sp),
                ).start()

        if it == ITERS - 1:
            deliver(STEPS)

        @pl.when(keeps)
        def _():
            arrived(incoming.at[pl.ds(0, SLICES - 1)], sc_recv.at[it, 0])
            errors = dot32(toep[...], incoming[...].reshape(SLICES * Q, ENS))
            if it:
                arrived(e_buf.at[pl.ds(0, 30)], sc_send.at[0, 1])
            e_buf[1:] = errors.reshape(SLICES, Q, ENS)

            @pl.loop(0, 16)
            def _(d):
                there = half * 16 + d

                @pl.when(there == j)
                def _():
                    got[own_brick] = e_buf[pl.ds(j, 2)]

                @pl.when(there != j)
                def _():
                    remote(
                        e_buf.at[pl.ds(there, 2)], got.at[own_brick],
                        sc_send.at[it, 1], sc_recv.at[it, 1], worker(there),
                    ).start()

            arrived(got.at[pl.ds(0, 7)], sc_recv.at[it, 1])
            arrived(incoming.at[pl.ds(0, 15)], sc_send.at[it, 0])

        @pl.when(moves)
        def _():
            arrived(got, sc_recv.at[it, 1])
            arrived(incoming.at[pl.ds(0, 16)], sc_send.at[it, 0])

        e_prev[...] += got[:, 0].reshape(HERE * Q, ENS)
        e_here[...] += got[:, 1].reshape(HERE * Q, ENS)
        prolong = restrict[...].T
        for g in range(2):
            part = slice(g * 4 * Q, (g + 1) * 4 * Q)
            ends[halves(g), :] = dot32(prolong, e_here[part, :])

        @pl.when(j == 0)
        def _():
            state[...] = start[...]

        @pl.when(j != 0)
        def _():
            for g in range(2):
                part = slice(g * 4 * Q, (g + 1) * 4 * Q)
                state[halves(g), :] = dot32(prolong, e_prev[part, :])

    stage[STEPS - 1] = ends[...].astype(BF16)
    deliver(STEPS - 1)
    for i in range(STEPS - 1):
        step(i)
        stage[i] = state[...].astype(BF16)
        deliver(i)

    @pl.when(keeps)
    def _():
        arrived(e_buf.at[pl.ds(0, 30)], sc_send.at[1, 1])

    @pl.when(moves)
    def _():
        arrived(home_nbr, swap_send.at[5])
        arrived(weights, swap_send.at[4])
        for i in range(STEPS):
            arrived(fields.at[i], swap_send.at[i])
        for n in range(STEPS + 1):
            arrived(stage.at[n], out_send.at[n])

    @pl.when((tm == 0) & (zh == 1))
    def _():
        arrived(start, swap_send.at[6])

    arrived(sol_ref, sol_recv)
    arrived(def_ref, def_recv)


def body(initial, forcing, brick_blocks, neighbours, coarse_modes, coarse_blocks):
    vmem = pl.BlockSpec(memory_space=pltpu.VMEM)
    hbm = pl.BlockSpec(memory_space=pl.ANY)
    sem = pltpu.SemaphoreType.DMA
    sol, last = pl.pallas_call(
        kernel,
        out_shape=(
            jax.ShapeDtypeStruct((STEPS, ROWS, ENS), BF16),
            jax.ShapeDtypeStruct((ROWS, ENS), BF16),
        ),
        in_specs=[hbm, hbm, hbm, vmem, vmem, vmem],
        out_specs=(hbm, hbm),
        scratch_shapes=[
            pltpu.VMEM((STEPS, ROWS, ENS), BF16),
            pltpu.VMEM((HERE, BRICK, (NB + 1) * BRICK), BF16),
            pltpu.VMEM((HERE, 128), jnp.int32),
            pltpu.VMEM((HERE, 128), jnp.int32),
            pltpu.VMEM((ROWS, ENS), F32),
            pltpu.VMEM((ROWS, ENS), F32),
            pltpu.VMEM((2, HALF, 3 * HALF), BF16),
            pltpu.VMEM((2, HALF, HALF), BF16),
            pltpu.VMEM((4 * HALF, ENS), BF16),
            pltpu.VMEM((4 * HALF, ENS), BF16),
            pltpu.VMEM((4 * Q, HALF), F32),
            pltpu.VMEM((SLICES * Q, SLICES * Q), F32),
            pltpu.VMEM((Q, 2 * SLICES * Q), F32),
            pltpu.VMEM((ITERS, HERE, Q, ENS), F32),
            pltpu.VMEM((SLICES, Q, ENS), F32),
            pltpu.VMEM((SLICES, Q, ENS), F32),
            pltpu.VMEM((SLICES + 1, Q, ENS), F32),
            pltpu.VMEM((HERE, 2, Q, ENS), F32),
            pltpu.VMEM((HERE, 2, Q, ENS), F32),
            pltpu.VMEM((HERE * Q, ENS), F32),
            pltpu.VMEM((HERE * Q, ENS), F32),
            pltpu.VMEM((ROWS, ENS), F32),
            pltpu.VMEM((STEPS + 1, ROWS, ENS), BF16),
            sem((STEPS,)),
            sem,
            sem,
            sem,
            sem((2, 2)),
            sem((2, 2)),
            sem((7,)),
            sem((ITERS, 2)),
            sem((ITERS, 2)),
            sem((STEPS + 1,)),
            sem,
            sem,
        ],
        compiler_params=pltpu.CompilerParams(
            collective_id=0, has_side_effects=True, vmem_limit_bytes=48 * 2**20
        ),
    )(
        initial.reshape(ROWS, ENS),
        forcing.reshape(STEPS, ROWS, ENS),
        brick_blocks,
        neighbours,
        coarse_modes,
        coarse_blocks,
    )
    return (
        sol.astype(F32).reshape(STEPS, HERE, BRICK, ENS),
        last.astype(F32).reshape(1, HERE, BRICK, ENS),
    )


def solution(mesh):
    placed = (
        P("space", None, None),
        P("tm", "space", None, None),
        P("space", None, None),
        P("space", None),
        P(),
        P("space", None, None),
    )
    return jax.shard_map(
        body,
        mesh=mesh,
        in_specs=placed,
        out_specs=(P("tm", "space", None, None), P("tm", "space", None, None)),
        check_vma=False,
    )
```

```python
import functools

import jax
import jax.numpy as jnp
from jax import lax
from jax.experimental import pallas as pl
from jax.experimental.pallas import tpu as pltpu
from jax.sharding import PartitionSpec as P

BRICK = 64
ENS = 128
NB = 6
REACH = 4
Q = 8
STEPS = 4
ITERS = 2
HERE = 8
SLICES = 32
ROWS = HERE * BRICK
HALF = ROWS // 2

MESH = pl.DeviceIdType.MESH
HIGHEST = lax.Precision.HIGHEST
F32 = jnp.float32
BF16 = jnp.bfloat16


def dot(a, b):
    return jnp.dot(a, b, preferred_element_type=F32)


def dot32(a, b):
    return jnp.dot(a, b, preferred_element_type=F32, precision=HIGHEST)


def kernel(
    init_ref, forcing_ref, blocks_ref, neighbours_ref, modes_ref, coarse_ref,
    sol_ref, def_ref,
    fields, weights, home_nbr, nbr, start, state, columns, band, diag, ext00, ext01, ext10, ext11,
    restrict, strip, toep_high, toep_low, r_buf, in0, in1, err0, err1, got0, got1, all0, all1,
    powers, held, stage,
    field_sem, weight_sem, nbr_sem, start_sem, halo_send, halo_recv, swap_send,
    sc_send, sc_recv, all_send, all_recv, power_send, power_recv, out_send, sol_recv, def_recv,
):
    tm = lax.axis_index("tm")
    sp = lax.axis_index("space")
    c = lax.rem(tm, 2)
    zl = lax.rem(tm // 2, 4)
    x = tm // 8
    y = sp // 2
    zh = lax.rem(sp, 2)
    keeps = c == zh
    moves = c != zh
    j = x * 8 + zl * 2 + zh
    q = 2 * y + c
    partner = (tm - c + zh, sp - zh + c)
    q_low = lax.rem(q + 7, 8)
    q_high = lax.rem(q + 1, 8)
    low = (tm - c + lax.rem(q_low, 2), (q_low // 2) * 2 + zh)
    high = (tm - c + lax.rem(q_high, 2), (q_high // 2) * 2 + zh)

    def worker(slice_id):
        return (
            (slice_id // 8) * 8 + lax.rem(slice_id // 2, 4) * 2 + c,
            2 * y + lax.rem(slice_id, 2),
        )

    def in_plane(other):
        return (tm - c + lax.rem(other, 2), (other // 2) * 2 + zh)

    @pl.when(keeps)
    def _():
        pltpu.make_async_copy(blocks_ref, weights, weight_sem).start()
        for i in range(STEPS):
            pltpu.make_async_copy(forcing_ref.at[i], fields.at[i], field_sem.at[i]).start()

    barrier = pltpu.get_barrier_semaphore()

    @pl.when(moves)
    def _():
        pl.semaphore_signal(barrier, inc=1, device_id=partner, device_id_type=MESH)

    @pl.loop(1, HERE)
    def _(d):
        pl.semaphore_signal(
            barrier, inc=1, device_id=in_plane(lax.rem(q + d, HERE)), device_id_type=MESH
        )

    @pl.loop(1, SLICES)
    def _(d):
        pl.semaphore_signal(
            barrier, inc=1, device_id=worker(lax.rem(j + d, SLICES)), device_id_type=MESH
        )

    home_nbr[...] = jnp.zeros_like(home_nbr)
    home_nbr[:, 0:NB] = neighbours_ref[...]
    peers = SLICES - 1 + HERE - 1
    pl.semaphore_wait(barrier, jnp.where(moves, peers + 1, peers))

    def remote(src, dst, send, recv, device):
        return pltpu.make_async_remote_copy(
            src_ref=src, dst_ref=dst, send_sem=send, recv_sem=recv,
            device_id=device, device_id_type=MESH,
        )

    def arrived(ref, sem):
        pltpu.make_async_copy(ref, ref, sem).wait()

    @pl.when(keeps)
    def _():
        pltpu.make_async_copy(home_nbr, nbr, nbr_sem).start()

    @pl.when(moves)
    def _():
        remote(home_nbr, nbr, swap_send.at[5], nbr_sem, partner).start()
        remote(blocks_ref, weights, swap_send.at[4], weight_sem, partner).start()
        for i in range(STEPS):
            remote(
                forcing_ref.at[i], fields.at[i], swap_send.at[i], field_sem.at[i], partner
            ).start()

    @pl.when((tm == 0) & (zh == 1))
    def _():
        remote(init_ref, start, swap_send.at[6], start_sem, partner).start()

    @pl.when((tm == 0) & (zh == 0))
    def _():
        pltpu.make_async_copy(init_ref, start, start_sem).start()

    modes = modes_ref[...]
    wide = jnp.concatenate([jnp.concatenate([modes] * 4, axis=1)] * 4, axis=0)
    row = lax.broadcasted_iota(jnp.int32, (4 * Q, HALF), 0)
    col = lax.broadcasted_iota(jnp.int32, (4 * Q, HALF), 1)
    restrict[...] = jnp.where(row // Q == col // BRICK, wide, 0.0)

    owns = keeps & (zl < 2)
    group = lax.rem(zl, 2)
    four = coarse_ref[pl.ds(4 * group, 4)].reshape(4 * Q, Q)
    row = lax.broadcasted_iota(jnp.int32, (4 * Q, 4 * Q), 0)
    col = lax.broadcasted_iota(jnp.int32, (4 * Q, 4 * Q), 1)
    power = jnp.where(row // Q == col // Q, jnp.concatenate([four] * 4, axis=1), 0.0)
    chain = (row == col).astype(F32)
    while chain.shape[1] < SLICES * 4 * Q:
        chain = jnp.concatenate([dot32(power, chain), chain], axis=1)
        power = dot32(power, power)
    strip[:, 0 : SLICES * 4 * Q] = chain
    strip[:, SLICES * 4 * Q :] = jnp.zeros((4 * Q, SLICES * 4 * Q), F32)
    near = strip[:, pl.ds(pl.multiple_of((3 - x) * 256, 256), 1280)]
    for d in range(9):
        first = (8 - d) * 4 * Q
        part = near[:, first : first + SLICES * 4 * Q]
        high_part = part.astype(BF16)
        toep_high[d * 4 * Q : (d + 1) * 4 * Q, :] = high_part
        toep_low[d * 4 * Q : (d + 1) * 4 * Q, :] = (part - high_part.astype(F32)).astype(BF16)

    tall = jnp.concatenate([modes] * 16, axis=0).T
    row = lax.broadcasted_iota(jnp.int32, (BRICK, ENS), 0) * 0 + 8 * c
    col = lax.broadcasted_iota(jnp.int32, (BRICK, ENS), 1) // Q
    for b in range(HERE):
        columns[b * BRICK : (b + 1) * BRICK, :] = jnp.where(
            (row + b == col) & (y == x), tall, 0.0
        )

    arrived(nbr, nbr_sem)
    arrived(weights, weight_sem)
    brick_ids = lax.broadcasted_iota(jnp.int32, (HERE, 128), 0)
    shift = lax.rem(nbr[...] - (8 * q + brick_ids) + (REACH + 64), 64)
    nbr[...] = shift + lax.rem(brick_ids, 4)
    lane_brick = lax.broadcasted_iota(jnp.int32, (BRICK, 128), 1) // BRICK

    @pl.loop(0, HERE)
    def _(b):
        g, b4 = b // 4, lax.rem(b, 4)
        rows = pl.ds(pl.multiple_of(b4 * BRICK, BRICK), BRICK)
        places = nbr[pl.ds(b, 1), :]
        where = [jnp.broadcast_to(places[:, k : k + 1], (BRICK, 128)) for k in range(NB)]
        twice = []
        for k in range(NB + 1):
            block = weights[b, :, k * BRICK : (k + 1) * BRICK].astype(F32)
            twice.append(jnp.concatenate([block, block], axis=1))
        for pair in range(6):
            there = lane_brick + 2 * pair
            block = jnp.zeros((BRICK, 128), F32)
            for k in range(NB):
                block = jnp.where(where[k] == there, twice[k + 1], block)
            band[g, rows, pair * 128 : (pair + 1) * 128] = block.astype(BF16)
        for pair in range(2):
            block = jnp.where(lane_brick + 2 * pair == b4, twice[0], 0.0)
            diag[g, rows, pair * 128 : (pair + 1) * 128] = block.astype(BF16)

    exts = ((ext00, ext01), (ext10, ext11))

    def halo(u, sweep):
        ext = exts[u][sweep]
        down = remote(
            ext.at[pl.ds(HALF, HALF)], ext.at[pl.ds(3 * HALF, HALF)],
            halo_send.at[u, sweep, 0], halo_recv.at[u, sweep, 0], low,
        )
        up = remote(
            ext.at[pl.ds(2 * HALF, HALF)], ext.at[pl.ds(0, HALF)],
            halo_send.at[u, sweep, 1], halo_recv.at[u, sweep, 1], high,
        )
        return down, up

    def begin(u, sweep, values):
        ext = exts[u][sweep]
        down, up = halo(u, sweep)
        ext[HALF : 2 * HALF, :] = dot(diag[0], values[0].astype(BF16)).astype(BF16)
        down.start()
        ext[2 * HALF : 3 * HALF, :] = dot(diag[1], values[1].astype(BF16)).astype(BF16)
        up.start()

    def end(u, sweep, values):
        ext = exts[u][sweep]
        near = (
            dot(band[0, :, HALF:], ext[HALF : 3 * HALF, :]),
            dot(band[1, :, : 2 * HALF], ext[HALF : 3 * HALF, :]),
        )
        down, up = halo(u, sweep)
        down.wait_send()
        up.wait_send()
        down.wait_recv()
        up.wait_recv()
        return (
            values[0] - near[0] - dot(band[0, :, :HALF], ext[0:HALF, :]),
            values[1] - near[1] - dot(band[1, :, 2 * HALF :], ext[3 * HALF :, :]),
        )

    def halves(g):
        return slice(g * HALF, (g + 1) * HALF)

    def deliver(n):
        target = sol_ref.at[n] if n < STEPS else def_ref

        @pl.when(keeps)
        def _():
            pltpu.make_async_copy(
                stage.at[n], target, sol_recv if n < STEPS else def_recv
            ).start()

        @pl.when(moves)
        def _():
            remote(
                stage.at[n], target, out_send.at[n], sol_recv if n < STEPS else def_recv, partner
            ).start()

    def share(i):
        for d in range(1, 4):
            remote(
                powers.at[i, x], powers.at[i, x], power_send.at[i], power_recv.at[i],
                (lax.rem(x + d, 4) * 8 + zl * 2 + c, sp),
            ).start()

    @pl.when(j == 0)
    def _():
        arrived(start, start_sem)
        state[...] = start[...]

    @pl.when(j != 0)
    def _():
        state[...] = jnp.zeros_like(state)

    @pl.loop(0, STEPS)
    def _(i):
        refs = (state, columns)

        def values(u):
            return refs[u][0:HALF, :], refs[u][HALF:ROWS, :]

        begin(0, 0, values(0))
        begin(1, 0, values(1))
        begin(0, 1, end(0, 0, values(0)))
        begin(1, 1, end(1, 0, values(1)))
        last = end(0, 1, values(0))
        arrived(fields.at[i], field_sem.at[i])
        for g in range(2):
            following = dot(diag[g], last[g].astype(BF16)) + fields[i, halves(g), :].astype(F32)
            state[halves(g), :] = following
            held[i, halves(g), :] = following
        last = end(1, 1, values(1))
        for g in range(2):
            following = dot(diag[g], last[g].astype(BF16))
            columns[halves(g), :] = following
            powers[i, x, halves(g), :] = following.astype(BF16)

        @pl.when(i < STEPS - 1)
        def _():
            share(i)

    prolong = restrict[...].T

    def coarse_part(i, gathered, g):
        matrix = jnp.concatenate([powers[i, n, halves(g), :] for n in range(4)], axis=1)
        return dot(matrix, gathered[...])

    sum_prev = sum_here = None
    for it, (incoming, err, got, gathered) in enumerate(
        ((in0, err0, got0, all0), (in1, err1, got1, all1))
    ):
        for g in range(2):
            defect = state[halves(g), :]
            if it:
                defect += coarse_part(STEPS - 1, all0, g)
                defect -= dot32(prolong, sum_here[g])
                stage[STEPS, halves(g), :] = defect.astype(BF16)
            r_buf[it, g] = dot32(restrict[...], defect).astype(BF16)

        @pl.loop(0, 8)
        def _(w):
            g = lax.rem(w, 2)
            owner_tm = (w // 2) * 8 + g * 2 + c
            owner_sp = 2 * y + c
            mine = (owner_tm == tm) & (owner_sp == sp)

            @pl.when(mine)
            def _():
                incoming[j] = r_buf[it, g]

            @pl.when(jnp.logical_not(mine))
            def _():
                remote(
                    r_buf.at[it, g], incoming.at[j], sc_send.at[it, 0], sc_recv.at[it, 0],
                    (owner_tm, owner_sp),
                ).start()

        if it:
            deliver(STEPS)
        else:
            share(STEPS - 1)

        @pl.when(owns)
        def _():
            arrived(incoming.at[pl.ds(0, SLICES - 1)], sc_recv.at[it, 0])
            terms = incoming[...].reshape(SLICES * 4 * Q, ENS)
            errors = dot(toep_high[...], terms) + dot(toep_low[...], terms)
            err[...] = errors.astype(BF16).reshape(9, 4 * Q, ENS)

            @pl.loop(0, 8)
            def _(d):
                there = x * 8 + d

                @pl.when(there == j)
                def _():
                    got[group] = err[pl.ds(d, 2)]

                @pl.when(there != j)
                def _():
                    remote(
                        err.at[pl.ds(d, 2)], got.at[group],
                        sc_send.at[it, 1], sc_recv.at[it, 1], worker(there),
                    ).start()

            arrived(got.at[0], sc_recv.at[it, 1])

        @pl.when(jnp.logical_not(owns))
        def _():
            arrived(got, sc_recv.at[it, 1])

        e_prev = [got[g, 0].astype(F32) for g in range(2)]
        e_here = [got[g, 1].astype(F32) for g in range(2)]
        if it:
            e_prev = [a + b for a, b in zip(e_prev, sum_prev)]
            e_here = [a + b for a, b in zip(e_here, sum_here)]
        sum_prev, sum_here = e_prev, e_here
        mine = pl.ds(pl.multiple_of(q * HERE * Q, HERE * Q), HERE * Q)
        gathered[mine, :] = jnp.concatenate(sum_prev, axis=0).astype(BF16)

        @pl.loop(1, HERE)
        def _(d):
            remote(
                gathered.at[mine], gathered.at[mine], all_send.at[it], all_recv.at[it],
                in_plane(lax.rem(q + d, HERE)),
            ).start()

        if it:
            for g in range(2):
                stage[STEPS - 1, halves(g), :] = dot32(prolong, sum_here[g]).astype(BF16)
            deliver(STEPS - 1)
        else:
            arrived(powers.at[STEPS - 1, pl.ds(0, 3)], power_recv.at[STEPS - 1])
        arrived(gathered.at[pl.ds(0, 7 * HERE * Q)], all_recv.at[it])

    for i in range(STEPS - 1):
        arrived(powers.at[i, pl.ds(0, 3)], power_recv.at[i])
        for g in range(2):
            stage[i, halves(g), :] = (held[i, halves(g), :] + coarse_part(i, all1, g)).astype(BF16)
        deliver(i)

    for it, (incoming, got) in enumerate(((in0, got0), (in1, got1))):
        arrived(all0.at[pl.ds(0, 7 * HERE * Q)], all_send.at[it])

        @pl.when(owns)
        def _():
            arrived(incoming.at[pl.ds(0, 7)], sc_send.at[it, 0])
            arrived(incoming.at[pl.ds(0, 14)], sc_send.at[it, 1])

        @pl.when(jnp.logical_not(owns))
        def _():
            arrived(incoming.at[pl.ds(0, 8)], sc_send.at[it, 0])

    for i in range(STEPS):
        arrived(powers.at[i, pl.ds(0, 3)], power_send.at[i])

    @pl.when(moves)
    def _():
        arrived(home_nbr, swap_send.at[5])
        arrived(weights, swap_send.at[4])
        for i in range(STEPS):
            arrived(fields.at[i], swap_send.at[i])
        for n in range(STEPS + 1):
            arrived(stage.at[n], out_send.at[n])

    @pl.when((tm == 0) & (zh == 1))
    def _():
        arrived(start, swap_send.at[6])

    arrived(sol_ref, sol_recv)
    arrived(def_ref, def_recv)


def body(initial, forcing, brick_blocks, neighbours, coarse_modes, coarse_blocks):
    vmem = pl.BlockSpec(memory_space=pltpu.VMEM)
    hbm = pl.BlockSpec(memory_space=pl.ANY)
    sem = pltpu.SemaphoreType.DMA
    sol, last = pl.pallas_call(
        kernel,
        out_shape=(
            jax.ShapeDtypeStruct((STEPS, ROWS, ENS), BF16),
            jax.ShapeDtypeStruct((ROWS, ENS), BF16),
        ),
        in_specs=[hbm, hbm, hbm, vmem, vmem, vmem],
        out_specs=(hbm, hbm),
        scratch_shapes=[
            pltpu.VMEM((STEPS, ROWS, ENS), BF16),
            pltpu.VMEM((HERE, BRICK, (NB + 1) * BRICK), BF16),
            pltpu.VMEM((HERE, 128), jnp.int32),
            pltpu.VMEM((HERE, 128), jnp.int32),
            pltpu.VMEM((ROWS, ENS), F32),
            pltpu.VMEM((ROWS, ENS), F32),
            pltpu.VMEM((ROWS, ENS), F32),
            pltpu.VMEM((2, HALF, 3 * HALF), BF16),
            pltpu.VMEM((2, HALF, HALF), BF16),
            *[pltpu.VMEM((4 * HALF, ENS), BF16)] * 4,
            pltpu.VMEM((4 * Q, HALF), F32),
            pltpu.VMEM((4 * Q, 2 * SLICES * 4 * Q), F32),
            pltpu.VMEM((9 * 4 * Q, SLICES * 4 * Q), BF16),
            pltpu.VMEM((9 * 4 * Q, SLICES * 4 * Q), BF16),
            pltpu.VMEM((ITERS, 2, 4 * Q, ENS), BF16),
            *[pltpu.VMEM((SLICES, 4 * Q, ENS), BF16)] * 2,
            *[pltpu.VMEM((9, 4 * Q, ENS), BF16)] * 2,
            *[pltpu.VMEM((2, 2, 4 * Q, ENS), BF16)] * 2,
            *[pltpu.VMEM((HERE * HERE * Q, ENS), BF16)] * 2,
            pltpu.VMEM((STEPS, 4, ROWS, ENS), BF16),
            pltpu.VMEM((STEPS, ROWS, ENS), F32),
            pltpu.VMEM((STEPS + 1, ROWS, ENS), BF16),
            sem((STEPS,)),
            sem,
            sem,
            sem,
            sem((2, 2, 2)),
            sem((2, 2, 2)),
            sem((7,)),
            sem((ITERS, 2)),
            sem((ITERS, 2)),
            sem((ITERS,)),
            sem((ITERS,)),
            sem((STEPS,)),
            sem((STEPS,)),
            sem((STEPS + 1,)),
            sem,
            sem,
        ],
        compiler_params=pltpu.CompilerParams(
            collective_id=0, has_side_effects=True, vmem_limit_bytes=60 * 2**20
        ),
    )(
        initial.reshape(ROWS, ENS),
        forcing.reshape(STEPS, ROWS, ENS),
        brick_blocks,
        neighbours,
        coarse_modes,
        coarse_blocks,
    )
    return (
        sol.astype(F32).reshape(STEPS, HERE, BRICK, ENS),
        last.astype(F32).reshape(1, HERE, BRICK, ENS),
    )


def solution(mesh):
    placed = (
        P("space", None, None),
        P("tm", "space", None, None),
        P("space", None, None),
        P("space", None),
        P(),
        P("space", None, None),
    )
    return jax.shard_map(
        body,
        mesh=mesh,
        in_specs=placed,
        out_specs=(P("tm", "space", None, None), P("tm", "space", None, None)),
        check_vma=False,
    )
```

```python
import functools

import jax
import jax.numpy as jnp
from jax import lax
from jax.experimental import pallas as pl
from jax.experimental.pallas import tpu as pltpu
from jax.sharding import PartitionSpec as P

BRICK = 64
ENS = 128
NB = 6
REACH = 4
Q = 8
STEPS = 4
ITERS = 2
HERE = 8
SLICES = 32
ROWS = HERE * BRICK
HALF = ROWS // 2

MESH = pl.DeviceIdType.MESH
HIGHEST = lax.Precision.HIGHEST
F32 = jnp.float32
BF16 = jnp.bfloat16


def dot(a, b):
    return jnp.dot(a, b, preferred_element_type=F32)


def dot32(a, b):
    return jnp.dot(a, b, preferred_element_type=F32, precision=HIGHEST)


def kernel(
    init_ref, forcing_ref, blocks_ref, neighbours_ref, modes_ref, coarse_ref,
    sol_ref, def_ref,
    fields, weights, home_nbr, nbr, start, state, columns, band, diag, ext00, ext01, ext10, ext11,
    restrict, strip, toep_high, toep_low, r_buf, in0, in1, err0, err1, got0, got1, all0, all1,
    powers, held, stage,
    field_sem, weight_sem, nbr_sem, start_sem, halo_send, halo_recv, swap_send, row_send, row_recv,
    sc_send, sc_recv, all_send, all_recv, power_send, power_recv, out_send, sol_recv, def_recv,
):
    tm = lax.axis_index("tm")
    sp = lax.axis_index("space")
    c = lax.rem(tm, 2)
    zl = lax.rem(tm // 2, 4)
    x = tm // 8
    y = sp // 2
    zh = lax.rem(sp, 2)
    keeps = c == zh
    moves = c != zh
    j = x * 8 + zl * 2 + zh
    q = 2 * y + c
    partner = (tm - c + zh, sp - zh + c)
    slow, fast = c, 1 - c

    def worker(slice_id):
        return (
            (slice_id // 8) * 8 + lax.rem(slice_id // 2, 4) * 2 + c,
            2 * y + lax.rem(slice_id, 2),
        )

    def in_plane(other):
        return (tm - c + lax.rem(other, 2), (other // 2) * 2 + zh)

    @pl.when(keeps)
    def _():
        pltpu.make_async_copy(blocks_ref, weights, weight_sem).start()
        for i in range(STEPS):
            pltpu.make_async_copy(forcing_ref.at[i], fields.at[i], field_sem.at[i]).start()

    barrier = pltpu.get_barrier_semaphore()

    @pl.when(moves)
    def _():
        pl.semaphore_signal(barrier, inc=1, device_id=partner, device_id_type=MESH)

    @pl.loop(1, HERE)
    def _(d):
        pl.semaphore_signal(
            barrier, inc=1, device_id=in_plane(lax.rem(q + d, HERE)), device_id_type=MESH
        )

    @pl.loop(1, SLICES)
    def _(d):
        pl.semaphore_signal(
            barrier, inc=1, device_id=worker(lax.rem(j + d, SLICES)), device_id_type=MESH
        )

    home_nbr[...] = jnp.zeros_like(home_nbr)
    home_nbr[:, 0:NB] = neighbours_ref[...]
    peers = SLICES - 1 + HERE - 1
    pl.semaphore_wait(barrier, jnp.where(moves, peers + 1, peers))

    def remote(src, dst, send, recv, device):
        return pltpu.make_async_remote_copy(
            src_ref=src, dst_ref=dst, send_sem=send, recv_sem=recv,
            device_id=device, device_id_type=MESH,
        )

    def arrived(ref, sem):
        pltpu.make_async_copy(ref, ref, sem).wait()

    @pl.when(keeps)
    def _():
        pltpu.make_async_copy(home_nbr, nbr, nbr_sem).start()

    def field(i):
        return remote(
            forcing_ref.at[i], fields.at[i], swap_send.at[i], field_sem.at[i], partner
        )

    fetched = pl.ds(2 * x, 2)

    @pl.when(moves)
    def _():
        remote(home_nbr, nbr, swap_send.at[5], nbr_sem, partner).start()
        remote(
            blocks_ref.at[fetched], weights.at[fetched], swap_send.at[4], weight_sem, partner
        ).start()

    @pl.when((tm == 0) & (zh == 1))
    def _():
        remote(init_ref, start, swap_send.at[6], start_sem, partner).start()

    @pl.when((tm == 0) & (zh == 0))
    def _():
        pltpu.make_async_copy(init_ref, start, start_sem).start()

    modes = modes_ref[...]
    wide = jnp.concatenate([jnp.concatenate([modes] * 4, axis=1)] * 4, axis=0)
    row = lax.broadcasted_iota(jnp.int32, (4 * Q, HALF), 0)
    col = lax.broadcasted_iota(jnp.int32, (4 * Q, HALF), 1)
    restrict[...] = jnp.where(row // Q == col // BRICK, wide, 0.0)

    owns = keeps & (zl < 2)
    group = lax.rem(zl, 2)
    four = coarse_ref[pl.ds(4 * group, 4)].reshape(4 * Q, Q)
    row = lax.broadcasted_iota(jnp.int32, (4 * Q, 4 * Q), 0)
    col = lax.broadcasted_iota(jnp.int32, (4 * Q, 4 * Q), 1)
    power = jnp.where(row // Q == col // Q, jnp.concatenate([four] * 4, axis=1), 0.0)
    chain = (row == col).astype(F32)
    while chain.shape[1] < SLICES * 4 * Q:
        chain = jnp.concatenate([dot32(power, chain), chain], axis=1)
        power = dot32(power, power)
    strip[:, 0 : SLICES * 4 * Q] = chain
    strip[:, SLICES * 4 * Q :] = jnp.zeros((4 * Q, SLICES * 4 * Q), F32)
    near = strip[:, pl.ds(pl.multiple_of((3 - x) * 256, 256), 1280)]
    for d in range(9):
        first = (8 - d) * 4 * Q
        part = near[:, first : first + SLICES * 4 * Q]
        high_part = part.astype(BF16)
        toep_high[d * 4 * Q : (d + 1) * 4 * Q, :] = high_part
        toep_low[d * 4 * Q : (d + 1) * 4 * Q, :] = (part - high_part.astype(F32)).astype(BF16)

    tall = jnp.concatenate([modes] * 16, axis=0).T
    row = lax.broadcasted_iota(jnp.int32, (BRICK, ENS), 0) * 0 + 8 * c
    col = lax.broadcasted_iota(jnp.int32, (BRICK, ENS), 1) // Q
    for b in range(HERE):
        columns[b * BRICK : (b + 1) * BRICK, :] = jnp.where(
            (row + b == col) & (y == x), tall, 0.0
        )

    arrived(nbr, nbr_sem)

    @pl.when(keeps)
    def _():
        arrived(weights, weight_sem)

    @pl.when(moves)
    def _():
        arrived(weights.at[pl.ds(0, 2)], weight_sem)
        for d in range(1, 4):
            remote(
                weights.at[fetched], weights.at[fetched], row_send, row_recv,
                (lax.rem(x + d, 4) * 8 + zl * 2 + c, sp),
            ).start()
        field(0).start()
        field(1).start()
        arrived(weights.at[pl.ds(0, 6)], row_recv)

    brick_ids = lax.broadcasted_iota(jnp.int32, (HERE, 128), 0)
    shift = lax.rem(nbr[...] - (8 * q + brick_ids) + (REACH + 64), 64)
    window = shift + lax.rem(brick_ids, 4)
    nbr[...] = jnp.where(brick_ids < 4, lax.rem(window + 8, 12), window)
    lane_brick = lax.broadcasted_iota(jnp.int32, (BRICK, 128), 1) // BRICK

    @pl.loop(0, HERE)
    def _(b):
        g, b4 = b // 4, lax.rem(b, 4)
        rows = pl.ds(pl.multiple_of(b4 * BRICK, BRICK), BRICK)
        places = nbr[pl.ds(b, 1), :]
        where = [jnp.broadcast_to(places[:, k : k + 1], (BRICK, 128)) for k in range(NB)]
        twice = []
        for k in range(NB + 1):
            block = weights[b, :, k * BRICK : (k + 1) * BRICK].astype(F32)
            twice.append(jnp.concatenate([block, block], axis=1))
        for pair in range(6):
            there = lane_brick + 2 * pair
            block = jnp.zeros((BRICK, 128), F32)
            for k in range(NB):
                block = jnp.where(where[k] == there, twice[k + 1], block)
            band[g, rows, pair * 128 : (pair + 1) * 128] = block.astype(BF16)
        for pair in range(2):
            block = jnp.where(lane_brick + 2 * pair == b4, twice[0], 0.0)
            diag[g, rows, pair * 128 : (pair + 1) * 128] = block.astype(BF16)

    exts = ((ext00, ext01), (ext10, ext11))

    def rows_of(g):
        return pl.ds(pl.multiple_of(g * HALF, HALF), HALF)

    def halo(u, sweep, g):
        ext = exts[u][sweep]
        return remote(
            ext.at[rows_of(g)], ext.at[rows_of(3 - g)],
            halo_send.at[u, sweep, g], halo_recv.at[u, sweep, 1 - g],
            in_plane(lax.rem(q + 7 + 2 * g, HERE)),
        )

    def send_half(u, sweep, g, values):
        exts[u][sweep][rows_of(g), :] = dot(diag[g], values.astype(BF16)).astype(BF16)
        halo(u, sweep, g).start()

    def uncoupled(u, sweep, g):
        ext = exts[u][sweep]
        near = dot(band[g, :, : 2 * HALF], ext[0 : 2 * HALF, :])
        arrived(ext.at[rows_of(2 + g)], halo_recv.at[u, sweep, g])
        far = dot(band[g, :, 2 * HALF :], ext[rows_of(2 + g), :])
        return (state, columns)[u][rows_of(g), :] - near - far

    def halves(g):
        return slice(g * HALF, (g + 1) * HALF)

    def deliver(n):
        target = sol_ref.at[n] if n < STEPS else def_ref

        @pl.when(keeps)
        def _():
            pltpu.make_async_copy(
                stage.at[n], target, sol_recv if n < STEPS else def_recv
            ).start()

        @pl.when(moves)
        def _():
            remote(
                stage.at[n], target, out_send.at[n], sol_recv if n < STEPS else def_recv, partner
            ).start()

    def share(i):
        for d in range(1, 4):
            remote(
                powers.at[i, x], powers.at[i, x], power_send.at[i], power_recv.at[i],
                (lax.rem(x + d, 4) * 8 + zl * 2 + c, sp),
            ).start()

    @pl.when(j == 0)
    def _():
        arrived(start, start_sem)
        state[...] = start[...]

    @pl.when(j != 0)
    def _():
        state[...] = jnp.zeros_like(state)

    for u, ref in enumerate((state, columns)):
        for g in (slow, fast):
            send_half(u, 0, g, ref[rows_of(g), :])

    @pl.loop(0, STEPS)
    def _(i):
        @pl.when(moves & (i < 2))
        def _():
            field(i + 2).start()

        for g in (fast, slow):
            for u in range(2):
                send_half(u, 1, g, uncoupled(u, 0, g))
        arrived(fields.at[i], field_sem.at[i])
        for g in (fast, slow):
            for u in range(2):
                following = dot(diag[g], uncoupled(u, 1, g).astype(BF16))
                arrived(ext00.at[rows_of(0)], halo_send.at[u, 0, g])
                arrived(ext00.at[rows_of(0)], halo_send.at[u, 1, g])
                if u == 0:
                    following += fields[i, rows_of(g), :].astype(F32)
                    state[rows_of(g), :] = following
                    held[i, rows_of(g), :] = following
                else:
                    columns[rows_of(g), :] = following
                    powers[i, x, rows_of(g), :] = following.astype(BF16)

                @pl.when(i < STEPS - 1)
                def _():
                    send_half(u, 0, g, following)

        @pl.when(i < STEPS - 1)
        def _():
            share(i)

    prolong = restrict[...].T

    def coarse_part(i, gathered, g):
        matrix = jnp.concatenate([powers[i, n, halves(g), :] for n in range(4)], axis=1)
        return dot(matrix, gathered[...])

    sum_prev = sum_here = None
    for it, (incoming, err, got, gathered) in enumerate(
        ((in0, err0, got0, all0), (in1, err1, got1, all1))
    ):
        for g in range(2):
            defect = state[halves(g), :]
            if it:
                defect += coarse_part(STEPS - 1, all0, g)
                defect -= dot32(prolong, sum_here[g])
                stage[STEPS, halves(g), :] = defect.astype(BF16)
            r_buf[it, g] = dot32(restrict[...], defect).astype(BF16)

        @pl.loop(0, 8)
        def _(w):
            g = lax.rem(w, 2)
            owner_tm = (w // 2) * 8 + g * 2 + c
            owner_sp = 2 * y + c
            mine = (owner_tm == tm) & (owner_sp == sp)

            @pl.when(mine)
            def _():
                incoming[j] = r_buf[it, g]

            @pl.when(jnp.logical_not(mine))
            def _():
                remote(
                    r_buf.at[it, g], incoming.at[j], sc_send.at[it, 0], sc_recv.at[it, 0],
                    (owner_tm, owner_sp),
                ).start()

        if it:
            deliver(STEPS)
        else:
            share(STEPS - 1)

        @pl.when(owns)
        def _():
            arrived(incoming.at[pl.ds(0, SLICES - 1)], sc_recv.at[it, 0])
            terms = incoming[...].reshape(SLICES * 4 * Q, ENS)
            errors = dot(toep_high[...], terms) + dot(toep_low[...], terms)
            err[...] = errors.astype(BF16).reshape(9, 4 * Q, ENS)

            @pl.loop(0, 8)
            def _(d):
                there = x * 8 + d

                @pl.when(there == j)
                def _():
                    got[group] = err[pl.ds(d, 2)]

                @pl.when(there != j)
                def _():
                    remote(
                        err.at[pl.ds(d, 2)], got.at[group],
                        sc_send.at[it, 1], sc_recv.at[it, 1], worker(there),
                    ).start()

            arrived(got.at[0], sc_recv.at[it, 1])

        @pl.when(jnp.logical_not(owns))
        def _():
            arrived(got, sc_recv.at[it, 1])

        e_prev = [got[g, 0].astype(F32) for g in range(2)]
        e_here = [got[g, 1].astype(F32) for g in range(2)]
        if it:
            e_prev = [a + b for a, b in zip(e_prev, sum_prev)]
            e_here = [a + b for a, b in zip(e_here, sum_here)]
        sum_prev, sum_here = e_prev, e_here
        mine = pl.ds(pl.multiple_of(q * HERE * Q, HERE * Q), HERE * Q)
        gathered[mine, :] = jnp.concatenate(sum_prev, axis=0).astype(BF16)

        @pl.loop(1, HERE)
        def _(d):
            remote(
                gathered.at[mine], gathered.at[mine], all_send.at[it], all_recv.at[it],
                in_plane(lax.rem(q + d, HERE)),
            ).start()

        if it:
            for g in range(2):
                stage[STEPS - 1, halves(g), :] = dot32(prolong, sum_here[g]).astype(BF16)
            deliver(STEPS - 1)
        else:
            arrived(powers.at[STEPS - 1, pl.ds(0, 3)], power_recv.at[STEPS - 1])
        arrived(gathered.at[pl.ds(0, 7 * HERE * Q)], all_recv.at[it])

    for i in range(STEPS - 1):
        arrived(powers.at[i, pl.ds(0, 3)], power_recv.at[i])
        for g in range(2):
            stage[i, halves(g), :] = (held[i, halves(g), :] + coarse_part(i, all1, g)).astype(BF16)
        deliver(i)

    for it, (incoming, got) in enumerate(((in0, got0), (in1, got1))):
        arrived(all0.at[pl.ds(0, 7 * HERE * Q)], all_send.at[it])

        @pl.when(owns)
        def _():
            arrived(incoming.at[pl.ds(0, 7)], sc_send.at[it, 0])
            arrived(incoming.at[pl.ds(0, 14)], sc_send.at[it, 1])

        @pl.when(jnp.logical_not(owns))
        def _():
            arrived(incoming.at[pl.ds(0, 8)], sc_send.at[it, 0])

    for i in range(STEPS):
        arrived(powers.at[i, pl.ds(0, 3)], power_send.at[i])

    @pl.when(moves)
    def _():
        arrived(home_nbr, swap_send.at[5])
        arrived(weights.at[pl.ds(0, 2)], swap_send.at[4])
        arrived(weights.at[pl.ds(0, 6)], row_send)
        for i in range(STEPS):
            arrived(fields.at[i], swap_send.at[i])
        for n in range(STEPS + 1):
            arrived(stage.at[n], out_send.at[n])

    @pl.when((tm == 0) & (zh == 1))
    def _():
        arrived(start, swap_send.at[6])

    arrived(sol_ref, sol_recv)
    arrived(def_ref, def_recv)


def body(initial, forcing, brick_blocks, neighbours, coarse_modes, coarse_blocks):
    vmem = pl.BlockSpec(memory_space=pltpu.VMEM)
    hbm = pl.BlockSpec(memory_space=pl.ANY)
    sem = pltpu.SemaphoreType.DMA
    sol, last = pl.pallas_call(
        kernel,
        out_shape=(
            jax.ShapeDtypeStruct((STEPS, ROWS, ENS), BF16),
            jax.ShapeDtypeStruct((ROWS, ENS), BF16),
        ),
        in_specs=[hbm, hbm, hbm, vmem, vmem, vmem],
        out_specs=(hbm, hbm),
        scratch_shapes=[
            pltpu.VMEM((STEPS, ROWS, ENS), BF16),
            pltpu.VMEM((HERE, BRICK, (NB + 1) * BRICK), BF16),
            pltpu.VMEM((HERE, 128), jnp.int32),
            pltpu.VMEM((HERE, 128), jnp.int32),
            pltpu.VMEM((ROWS, ENS), F32),
            pltpu.VMEM((ROWS, ENS), F32),
            pltpu.VMEM((ROWS, ENS), F32),
            pltpu.VMEM((2, HALF, 3 * HALF), BF16),
            pltpu.VMEM((2, HALF, HALF), BF16),
            *[pltpu.VMEM((4 * HALF, ENS), BF16)] * 4,
            pltpu.VMEM((4 * Q, HALF), F32),
            pltpu.VMEM((4 * Q, 2 * SLICES * 4 * Q), F32),
            pltpu.VMEM((9 * 4 * Q, SLICES * 4 * Q), BF16),
            pltpu.VMEM((9 * 4 * Q, SLICES * 4 * Q), BF16),
            pltpu.VMEM((ITERS, 2, 4 * Q, ENS), BF16),
            *[pltpu.VMEM((SLICES, 4 * Q, ENS), BF16)] * 2,
            *[pltpu.VMEM((9, 4 * Q, ENS), BF16)] * 2,
            *[pltpu.VMEM((2, 2, 4 * Q, ENS), BF16)] * 2,
            *[pltpu.VMEM((HERE * HERE * Q, ENS), BF16)] * 2,
            pltpu.VMEM((STEPS, 4, ROWS, ENS), BF16),
            pltpu.VMEM((STEPS, ROWS, ENS), F32),
            pltpu.VMEM((STEPS + 1, ROWS, ENS), BF16),
            sem((STEPS,)),
            sem,
            sem,
            sem,
            sem((2, 2, 2)),
            sem((2, 2, 2)),
            sem((7,)),
            sem,
            sem,
            sem((ITERS, 2)),
            sem((ITERS, 2)),
            sem((ITERS,)),
            sem((ITERS,)),
            sem((STEPS,)),
            sem((STEPS,)),
            sem((STEPS + 1,)),
            sem,
            sem,
        ],
        compiler_params=pltpu.CompilerParams(
            collective_id=0, has_side_effects=True, vmem_limit_bytes=60 * 2**20
        ),
    )(
        initial.reshape(ROWS, ENS),
        forcing.reshape(STEPS, ROWS, ENS),
        brick_blocks,
        neighbours,
        coarse_modes,
        coarse_blocks,
    )
    return (
        sol.astype(F32).reshape(STEPS, HERE, BRICK, ENS),
        last.astype(F32).reshape(1, HERE, BRICK, ENS),
    )


def solution(mesh):
    placed = (
        P("space", None, None),
        P("tm", "space", None, None),
        P("space", None, None),
        P("space", None),
        P(),
        P("space", None, None),
    )
    return jax.shard_map(
        body,
        mesh=mesh,
        in_specs=placed,
        out_specs=(P("tm", "space", None, None), P("tm", "space", None, None)),
        check_vma=False,
    )
```

```python
import functools

import jax
import jax.numpy as jnp
from jax import lax
from jax.experimental import pallas as pl
from jax.experimental.pallas import tpu as pltpu
from jax.sharding import PartitionSpec as P

BRICK = 64
ENS = 128
NB = 6
REACH = 4
Q = 8
STEPS = 4
ITERS = 2
HERE = 8
SLICES = 32
ROWS = HERE * BRICK
HALF = ROWS // 2

MESH = pl.DeviceIdType.MESH
HIGHEST = lax.Precision.HIGHEST
F32 = jnp.float32
BF16 = jnp.bfloat16


def dot(a, b):
    return jnp.dot(a, b, preferred_element_type=F32)


def dot32(a, b):
    return jnp.dot(a, b, preferred_element_type=F32, precision=HIGHEST)


def kernel(
    init_ref, forcing_ref, blocks_ref, neighbours_ref, modes_ref, coarse_ref,
    sol_ref, def_ref,
    fields, weights, home_nbr, nbr, start, state, columns, band, diag, ext00, ext01, ext10, ext11,
    restrict, strip, toep_high, toep_low, r_buf, in0, in1, err0, err1, got0, got1, all0, all1,
    powers, home_powers, held, home_held, prev_buf, here_buf, home_here, stage,
    field_sem, weight_sem, nbr_sem, start_sem, halo_send, halo_recv, swap_send, row_send, row_recv,
    sc_send, sc_recv, all_send, all_recv, power_send, power_recv, forward_send, home_power_sem,
    held_send, home_held_sem, here_send, here_recv, out_send, sol_recv, def_recv,
):
    tm = lax.axis_index("tm")
    sp = lax.axis_index("space")
    c = lax.rem(tm, 2)
    zl = lax.rem(tm // 2, 4)
    x = tm // 8
    y = sp // 2
    zh = lax.rem(sp, 2)
    keeps = c == zh
    moves = c != zh
    j = x * 8 + zl * 2 + zh
    q = 2 * y + c
    partner = (tm - c + zh, sp - zh + c)
    slow, fast = c, 1 - c

    def worker(slice_id):
        return (
            (slice_id // 8) * 8 + lax.rem(slice_id // 2, 4) * 2 + c,
            2 * y + lax.rem(slice_id, 2),
        )

    def in_plane(other):
        return (tm - c + lax.rem(other, 2), (other // 2) * 2 + zh)

    @pl.when(keeps)
    def _():
        pltpu.make_async_copy(blocks_ref, weights, weight_sem).start()
        for i in range(STEPS):
            pltpu.make_async_copy(forcing_ref.at[i], fields.at[i], field_sem.at[i]).start()

    barrier = pltpu.get_barrier_semaphore()

    @pl.when(moves)
    def _():
        @pl.loop(0, HERE)
        def _(other):
            pl.semaphore_signal(
                barrier,
                inc=1,
                device_id=(tm - c + lax.rem(other, 2), (other // 2) * 2 + c),
                device_id_type=MESH,
            )

    @pl.loop(1, HERE)
    def _(d):
        pl.semaphore_signal(
            barrier, inc=1, device_id=in_plane(lax.rem(q + d, HERE)), device_id_type=MESH
        )

    @pl.loop(1, SLICES)
    def _(d):
        pl.semaphore_signal(
            barrier, inc=1, device_id=worker(lax.rem(j + d, SLICES)), device_id_type=MESH
        )

    home_nbr[...] = jnp.zeros_like(home_nbr)
    home_nbr[:, 0:NB] = neighbours_ref[...]
    pl.semaphore_wait(barrier, SLICES - 1 + HERE - 1 + HERE // 2)

    def remote(src, dst, send, recv, device):
        return pltpu.make_async_remote_copy(
            src_ref=src, dst_ref=dst, send_sem=send, recv_sem=recv,
            device_id=device, device_id_type=MESH,
        )

    def arrived(ref, sem):
        pltpu.make_async_copy(ref, ref, sem).wait()

    @pl.when(keeps)
    def _():
        pltpu.make_async_copy(home_nbr, nbr, nbr_sem).start()

    def field(i):
        return remote(
            forcing_ref.at[i], fields.at[i], swap_send.at[i], field_sem.at[i], partner
        )

    fetched = pl.ds(2 * x, 2)

    @pl.when(moves)
    def _():
        remote(home_nbr, nbr, swap_send.at[5], nbr_sem, partner).start()
        remote(
            blocks_ref.at[fetched], weights.at[fetched], swap_send.at[4], weight_sem, partner
        ).start()

    @pl.when((tm == 0) & (zh == 1))
    def _():
        remote(init_ref, start, swap_send.at[6], start_sem, partner).start()

    @pl.when((tm == 0) & (zh == 0))
    def _():
        pltpu.make_async_copy(init_ref, start, start_sem).start()

    modes = modes_ref[...]
    wide = jnp.concatenate([jnp.concatenate([modes] * 4, axis=1)] * 4, axis=0)
    row = lax.broadcasted_iota(jnp.int32, (4 * Q, HALF), 0)
    col = lax.broadcasted_iota(jnp.int32, (4 * Q, HALF), 1)
    restrict[...] = jnp.where(row // Q == col // BRICK, wide, 0.0)

    owns = keeps & (zl < 2)
    group = lax.rem(zl, 2)
    four = coarse_ref[pl.ds(4 * group, 4)].reshape(4 * Q, Q)
    row = lax.broadcasted_iota(jnp.int32, (4 * Q, 4 * Q), 0)
    col = lax.broadcasted_iota(jnp.int32, (4 * Q, 4 * Q), 1)
    power = jnp.where(row // Q == col // Q, jnp.concatenate([four] * 4, axis=1), 0.0)
    chain = (row == col).astype(F32)
    while chain.shape[1] < SLICES * 4 * Q:
        chain = jnp.concatenate([dot32(power, chain), chain], axis=1)
        power = dot32(power, power)
    strip[:, 0 : SLICES * 4 * Q] = chain
    strip[:, SLICES * 4 * Q :] = jnp.zeros((4 * Q, SLICES * 4 * Q), F32)
    near = strip[:, pl.ds(pl.multiple_of((3 - x) * 256, 256), 1280)]
    for d in range(9):
        first = (8 - d) * 4 * Q
        part = near[:, first : first + SLICES * 4 * Q]
        high_part = part.astype(BF16)
        toep_high[d * 4 * Q : (d + 1) * 4 * Q, :] = high_part
        toep_low[d * 4 * Q : (d + 1) * 4 * Q, :] = (part - high_part.astype(F32)).astype(BF16)

    tall = jnp.concatenate([modes] * 16, axis=0).T
    row = lax.broadcasted_iota(jnp.int32, (BRICK, ENS), 0) * 0 + 8 * c
    col = lax.broadcasted_iota(jnp.int32, (BRICK, ENS), 1) // Q
    for b in range(HERE):
        columns[b * BRICK : (b + 1) * BRICK, :] = jnp.where(
            (row + b == col) & (y == x), tall, 0.0
        )

    arrived(nbr, nbr_sem)

    @pl.when(keeps)
    def _():
        arrived(weights, weight_sem)

    @pl.when(moves)
    def _():
        arrived(weights.at[pl.ds(0, 2)], weight_sem)
        for d in range(1, 4):
            remote(
                weights.at[fetched], weights.at[fetched], row_send, row_recv,
                (lax.rem(x + d, 4) * 8 + zl * 2 + c, sp),
            ).start()
        field(0).start()
        field(1).start()
        arrived(weights.at[pl.ds(0, 6)], row_recv)

    brick_ids = lax.broadcasted_iota(jnp.int32, (HERE, 128), 0)
    shift = lax.rem(nbr[...] - (8 * q + brick_ids) + (REACH + 64), 64)
    window = shift + lax.rem(brick_ids, 4)
    nbr[...] = jnp.where(brick_ids < 4, lax.rem(window + 8, 12), window)
    lane_brick = lax.broadcasted_iota(jnp.int32, (BRICK, 128), 1) // BRICK

    @pl.loop(0, HERE)
    def _(b):
        g, b4 = b // 4, lax.rem(b, 4)
        rows = pl.ds(pl.multiple_of(b4 * BRICK, BRICK), BRICK)
        places = nbr[pl.ds(b, 1), :]
        where = [jnp.broadcast_to(places[:, k : k + 1], (BRICK, 128)) for k in range(NB)]
        twice = []
        for k in range(NB + 1):
            block = weights[b, :, k * BRICK : (k + 1) * BRICK].astype(F32)
            twice.append(jnp.concatenate([block, block], axis=1))
        for pair in range(6):
            there = lane_brick + 2 * pair
            block = jnp.zeros((BRICK, 128), F32)
            for k in range(NB):
                block = jnp.where(where[k] == there, twice[k + 1], block)
            band[g, rows, pair * 128 : (pair + 1) * 128] = block.astype(BF16)
        for pair in range(2):
            block = jnp.where(lane_brick + 2 * pair == b4, twice[0], 0.0)
            diag[g, rows, pair * 128 : (pair + 1) * 128] = block.astype(BF16)

    exts = ((ext00, ext01), (ext10, ext11))

    def rows_of(g):
        return pl.ds(pl.multiple_of(g * HALF, HALF), HALF)

    def halo(u, sweep, g):
        ext = exts[u][sweep]
        return remote(
            ext.at[rows_of(g)], ext.at[rows_of(3 - g)],
            halo_send.at[u, sweep, g], halo_recv.at[u, sweep, 1 - g],
            in_plane(lax.rem(q + 7 + 2 * g, HERE)),
        )

    def send_half(u, sweep, g, values):
        exts[u][sweep][rows_of(g), :] = dot(diag[g], values.astype(BF16)).astype(BF16)
        halo(u, sweep, g).start()

    def uncoupled(u, sweep, g):
        ext = exts[u][sweep]
        near = dot(band[g, :, : 2 * HALF], ext[0 : 2 * HALF, :])
        arrived(ext.at[rows_of(2 + g)], halo_recv.at[u, sweep, g])
        far = dot(band[g, :, 2 * HALF :], ext[rows_of(2 + g), :])
        return (state, columns)[u][rows_of(g), :] - near - far

    def halves(g):
        return slice(g * HALF, (g + 1) * HALF)

    def share(i):
        for d in range(1, 4):
            remote(
                powers.at[i, x], powers.at[i, x], power_send.at[i], power_recv.at[i],
                (lax.rem(x + d, 4) * 8 + zl * 2 + c, sp),
            ).start()

    def forward(i):
        arrived(powers.at[i, pl.ds(0, 3)], power_recv.at[i])
        pltpu.make_async_copy(powers.at[i], home_powers.at[i], home_power_sem.at[i]).start()
        remote(
            powers.at[i], home_powers.at[i], forward_send.at[i], home_power_sem.at[i],
            (tm - c + (1 - c), sp),
        ).start()

    def bring(source, target, send, recv):
        @pl.when(keeps)
        def _():
            pltpu.make_async_copy(source, target, recv).start()

        @pl.when(moves)
        def _():
            remote(source, target, send, recv, partner).start()

    @pl.when(j == 0)
    def _():
        arrived(start, start_sem)
        state[...] = start[...]

    @pl.when(j != 0)
    def _():
        state[...] = jnp.zeros_like(state)

    for u, ref in enumerate((state, columns)):
        for g in (slow, fast):
            send_half(u, 0, g, ref[rows_of(g), :])

    @pl.loop(0, STEPS)
    def _(i):
        @pl.when(moves & (i < 2))
        def _():
            field(i + 2).start()

        for g in (fast, slow):
            for u in range(2):
                send_half(u, 1, g, uncoupled(u, 0, g))
        arrived(fields.at[i], field_sem.at[i])
        for g in (fast, slow):
            for u in range(2):
                following = dot(diag[g], uncoupled(u, 1, g).astype(BF16))
                arrived(ext00.at[rows_of(0)], halo_send.at[u, 0, g])
                arrived(ext00.at[rows_of(0)], halo_send.at[u, 1, g])
                if u == 0:
                    following += fields[i, rows_of(g), :].astype(F32)
                    state[rows_of(g), :] = following
                    held[i, rows_of(g), :] = following.astype(BF16)
                else:
                    columns[rows_of(g), :] = following
                    powers[i, x, rows_of(g), :] = following.astype(BF16)

                @pl.when(i < STEPS - 1)
                def _():
                    send_half(u, 0, g, following)

        @pl.when(i < STEPS - 1)
        def _():
            bring(held.at[i], home_held.at[i], held_send.at[i], home_held_sem.at[i])

        @pl.when((i < STEPS - 1) & keeps)
        def _():
            share(i)

        @pl.when((i > 0) & keeps)
        def _():
            forward(i - 1)

    prolong = restrict[...].T

    def coarse_part(ref, i, gathered, g):
        matrix = jnp.concatenate([ref[i, n, halves(g), :] for n in range(4)], axis=1)
        return dot(matrix, gathered[...])

    sum_prev = sum_here = None
    for it, (incoming, err, got, gathered) in enumerate(
        ((in0, err0, got0, all0), (in1, err1, got1, all1))
    ):
        for g in range(2):
            defect = state[halves(g), :]
            if it:
                defect += coarse_part(powers, STEPS - 1, all0, g)
                defect -= dot32(prolong, sum_here[g])
                stage[STEPS, halves(g), :] = defect.astype(BF16)
            r_buf[it, g] = dot32(restrict[...], defect).astype(BF16)

        @pl.loop(0, 8)
        def _(w):
            g = lax.rem(w, 2)
            owner_tm = (w // 2) * 8 + g * 2 + c
            owner_sp = 2 * y + c
            mine = (owner_tm == tm) & (owner_sp == sp)

            @pl.when(mine)
            def _():
                incoming[j] = r_buf[it, g]

            @pl.when(jnp.logical_not(mine))
            def _():
                remote(
                    r_buf.at[it, g], incoming.at[j], sc_send.at[it, 0], sc_recv.at[it, 0],
                    (owner_tm, owner_sp),
                ).start()

        if it:
            bring(stage.at[STEPS], def_ref, out_send, def_recv)
        else:
            share(STEPS - 1)

        @pl.when(owns)
        def _():
            arrived(incoming.at[pl.ds(0, SLICES - 1)], sc_recv.at[it, 0])
            terms = incoming[...].reshape(SLICES * 4 * Q, ENS)
            errors = dot(toep_high[...], terms) + dot(toep_low[...], terms)
            err[...] = errors.astype(BF16).reshape(9, 4 * Q, ENS)

            @pl.loop(0, 8)
            def _(d):
                there = x * 8 + d

                @pl.when(there == j)
                def _():
                    got[group] = err[pl.ds(d, 2)]

                @pl.when(there != j)
                def _():
                    remote(
                        err.at[pl.ds(d, 2)], got.at[group],
                        sc_send.at[it, 1], sc_recv.at[it, 1], worker(there),
                    ).start()

            arrived(got.at[0], sc_recv.at[it, 1])

        @pl.when(jnp.logical_not(owns))
        def _():
            arrived(got, sc_recv.at[it, 1])

        e_prev = [got[g, 0].astype(F32) for g in range(2)]
        e_here = [got[g, 1].astype(F32) for g in range(2)]
        if it:
            e_prev = [a + b for a, b in zip(e_prev, sum_prev)]
            e_here = [a + b for a, b in zip(e_here, sum_here)]
        sum_prev, sum_here = e_prev, e_here
        mine = pl.ds(pl.multiple_of(q * HERE * Q, HERE * Q), HERE * Q)
        rounded_prev = jnp.concatenate(sum_prev, axis=0).astype(BF16)
        if it == 0:
            gathered[mine, :] = rounded_prev

            @pl.loop(1, HERE)
            def _(d):
                remote(
                    gathered.at[mine], gathered.at[mine], all_send.at[it], all_recv.at[it],
                    in_plane(lax.rem(q + d, HERE)),
                ).start()

            arrived(powers.at[STEPS - 1, pl.ds(0, 3)], power_recv.at[STEPS - 1])
            arrived(gathered.at[pl.ds(0, 7 * HERE * Q)], all_recv.at[it])
        else:
            prev_buf[...] = rounded_prev
            here_buf[...] = jnp.concatenate(sum_here, axis=0).astype(BF16)

            @pl.loop(0, HERE)
            def _(d):
                home = lax.rem(sp + d, HERE)
                own = keeps & (home == sp)

                @pl.when(own)
                def _():
                    gathered[mine, :] = prev_buf[...]

                @pl.when(jnp.logical_not(own))
                def _():
                    remote(
                        prev_buf, gathered.at[mine], all_send.at[it], all_recv.at[it],
                        (tm - c + zh, home),
                    ).start()

            bring(here_buf, home_here, here_send, here_recv)

    @pl.when(keeps)
    def _():
        arrived(all1.at[pl.ds(0, 7 * HERE * Q)], all_recv.at[1])

    @pl.when(moves)
    def _():
        arrived(all1, all_recv.at[1])

    for i in range(STEPS - 1):
        arrived(home_held.at[i], home_held_sem.at[i])
        arrived(home_powers.at[i], home_power_sem.at[i])
        for g in range(2):
            value = home_held[i, halves(g), :].astype(F32) + coarse_part(home_powers, i, all1, g)
            stage[i, halves(g), :] = value.astype(BF16)
        pltpu.make_async_copy(stage.at[i], sol_ref.at[i], sol_recv).start()
    arrived(home_here, here_recv)
    for g in range(2):
        part = home_here[g * 4 * Q : (g + 1) * 4 * Q, :].astype(F32)
        stage[STEPS - 1, halves(g), :] = dot32(prolong, part).astype(BF16)
    pltpu.make_async_copy(stage.at[STEPS - 1], sol_ref.at[STEPS - 1], sol_recv).start()

    for it, incoming in enumerate((in0, in1)):

        @pl.when(owns)
        def _():
            arrived(incoming.at[pl.ds(0, 7)], sc_send.at[it, 0])
            arrived(incoming.at[pl.ds(0, 14)], sc_send.at[it, 1])

        @pl.when(jnp.logical_not(owns))
        def _():
            arrived(incoming.at[pl.ds(0, 8)], sc_send.at[it, 0])

    arrived(all0.at[pl.ds(0, 7 * HERE * Q)], all_send.at[0])
    arrived(powers.at[STEPS - 1, pl.ds(0, 3)], power_send.at[STEPS - 1])

    @pl.when(keeps)
    def _():
        arrived(all0.at[pl.ds(0, 7 * HERE * Q)], all_send.at[1])
        for i in range(STEPS - 1):
            arrived(powers.at[i, pl.ds(0, 3)], power_send.at[i])
            arrived(powers.at[i], forward_send.at[i])

    @pl.when(moves)
    def _():
        arrived(all0, all_send.at[1])
        arrived(home_nbr, swap_send.at[5])
        arrived(weights.at[pl.ds(0, 2)], swap_send.at[4])
        arrived(weights.at[pl.ds(0, 6)], row_send)
        for i in range(STEPS):
            arrived(fields.at[i], swap_send.at[i])
        for i in range(STEPS - 1):
            arrived(held.at[i], held_send.at[i])
        arrived(stage.at[STEPS], out_send)
        arrived(here_buf, here_send)

    @pl.when((tm == 0) & (zh == 1))
    def _():
        arrived(start, swap_send.at[6])

    arrived(sol_ref, sol_recv)
    arrived(def_ref, def_recv)


def body(initial, forcing, brick_blocks, neighbours, coarse_modes, coarse_blocks):
    vmem = pl.BlockSpec(memory_space=pltpu.VMEM)
    hbm = pl.BlockSpec(memory_space=pl.ANY)
    sem = pltpu.SemaphoreType.DMA
    sol, last = pl.pallas_call(
        kernel,
        out_shape=(
            jax.ShapeDtypeStruct((STEPS, ROWS, ENS), BF16),
            jax.ShapeDtypeStruct((ROWS, ENS), BF16),
        ),
        in_specs=[hbm, hbm, hbm, vmem, vmem, vmem],
        out_specs=(hbm, hbm),
        scratch_shapes=[
            pltpu.VMEM((STEPS, ROWS, ENS), BF16),
            pltpu.VMEM((HERE, BRICK, (NB + 1) * BRICK), BF16),
            pltpu.VMEM((HERE, 128), jnp.int32),
            pltpu.VMEM((HERE, 128), jnp.int32),
            pltpu.VMEM((ROWS, ENS), F32),
            pltpu.VMEM((ROWS, ENS), F32),
            pltpu.VMEM((ROWS, ENS), F32),
            pltpu.VMEM((2, HALF, 3 * HALF), BF16),
            pltpu.VMEM((2, HALF, HALF), BF16),
            *[pltpu.VMEM((4 * HALF, ENS), BF16)] * 4,
            pltpu.VMEM((4 * Q, HALF), F32),
            pltpu.VMEM((4 * Q, 2 * SLICES * 4 * Q), F32),
            pltpu.VMEM((9 * 4 * Q, SLICES * 4 * Q), BF16),
            pltpu.VMEM((9 * 4 * Q, SLICES * 4 * Q), BF16),
            pltpu.VMEM((ITERS, 2, 4 * Q, ENS), BF16),
            *[pltpu.VMEM((SLICES, 4 * Q, ENS), BF16)] * 2,
            *[pltpu.VMEM((9, 4 * Q, ENS), BF16)] * 2,
            *[pltpu.VMEM((2, 2, 4 * Q, ENS), BF16)] * 2,
            *[pltpu.VMEM((HERE * HERE * Q, ENS), BF16)] * 2,
            pltpu.VMEM((STEPS, 4, ROWS, ENS), BF16),
            pltpu.VMEM((STEPS - 1, 4, ROWS, ENS), BF16),
            pltpu.VMEM((STEPS, ROWS, ENS), BF16),
            pltpu.VMEM((STEPS - 1, ROWS, ENS), BF16),
            *[pltpu.VMEM((HERE * Q, ENS), BF16)] * 3,
            pltpu.VMEM((STEPS + 1, ROWS, ENS), BF16),
            sem((STEPS,)),
            sem,
            sem,
            sem,
            sem((2, 2, 2)),
            sem((2, 2, 2)),
            sem((7,)),
            sem,
            sem,
            sem((ITERS, 2)),
            sem((ITERS, 2)),
            sem((ITERS,)),
            sem((ITERS,)),
            sem((STEPS,)),
            sem((STEPS,)),
            sem((STEPS - 1,)),
            sem((STEPS - 1,)),
            sem((STEPS - 1,)),
            sem((STEPS - 1,)),
            sem,
            sem,
            sem,
            sem,
            sem,
        ],
        compiler_params=pltpu.CompilerParams(
            collective_id=0, has_side_effects=True, vmem_limit_bytes=60 * 2**20
        ),
    )(
        initial.reshape(ROWS, ENS),
        forcing.reshape(STEPS, ROWS, ENS),
        brick_blocks,
        neighbours,
        coarse_modes,
        coarse_blocks,
    )
    return (
        sol.astype(F32).reshape(STEPS, HERE, BRICK, ENS),
        last.astype(F32).reshape(1, HERE, BRICK, ENS),
    )


def solution(mesh):
    placed = (
        P("space", None, None),
        P("tm", "space", None, None),
        P("space", None, None),
        P("space", None),
        P(),
        P("space", None, None),
    )
    return jax.shard_map(
        body,
        mesh=mesh,
        in_specs=placed,
        out_specs=(P("tm", "space", None, None), P("tm", "space", None, None)),
        check_vma=False,
    )
```

```python
import functools

import jax
import jax.numpy as jnp
from jax import lax
from jax.experimental import pallas as pl
from jax.experimental.pallas import tpu as pltpu
from jax.sharding import PartitionSpec as P

BRICK = 64
ENS = 128
NB = 6
REACH = 4
Q = 8
STEPS = 4
ITERS = 2
HERE = 8
SLICES = 32
ROWS = HERE * BRICK
HALF = ROWS // 2

MESH = pl.DeviceIdType.MESH
HIGHEST = lax.Precision.HIGHEST
F32 = jnp.float32
BF16 = jnp.bfloat16


def dot(a, b):
    return jnp.dot(a, b, preferred_element_type=F32)


def dot32(a, b):
    return jnp.dot(a, b, preferred_element_type=F32, precision=HIGHEST)


def kernel(
    init_ref, forcing_ref, blocks_ref, neighbours_ref, modes_ref, coarse_ref,
    sol_ref, def_ref,
    fields, weights, home_nbr, nbr, start, state, columns, band, folded, diag, ext00, ext01, ext10, ext11,
    restrict, prolong, strip, toep_high, toep_low, r_buf, in0, in1, err0, err1, got0, got1, all0, all1,
    powers, home_powers, held, home_held, prev_buf, here_buf, home_here, stage,
    field_sem, weight_sem, far_sem, nbr_sem, start_sem, halo_send, halo_recv, swap_send, row_send, row_recv,
    sc_send, sc_recv, all_send, all_recv, power_send, power_recv, forward_send, home_power_sem,
    held_send, home_held_sem, here_send, here_recv, out_send, sol_recv, def_recv,
):
    tm = lax.axis_index("tm")
    sp = lax.axis_index("space")
    c = lax.rem(tm, 2)
    zl = lax.rem(tm // 2, 4)
    x = tm // 8
    y = sp // 2
    zh = lax.rem(sp, 2)
    keeps = c == zh
    moves = c != zh
    j = x * 8 + zl * 2 + zh
    q = 2 * y + c
    partner = (tm - c + zh, sp - zh + c)
    slow, fast = c, 1 - c

    def worker(slice_id):
        return (
            (slice_id // 8) * 8 + lax.rem(slice_id // 2, 4) * 2 + c,
            2 * y + lax.rem(slice_id, 2),
        )

    def in_plane(other):
        return (tm - c + lax.rem(other, 2), (other // 2) * 2 + zh)

    @pl.when(keeps)
    def _():
        pltpu.make_async_copy(blocks_ref, weights, weight_sem).start()
        for i in range(STEPS):
            pltpu.make_async_copy(forcing_ref.at[i], fields.at[i], field_sem.at[i]).start()

    barrier = pltpu.get_barrier_semaphore()

    @pl.when(moves)
    def _():
        @pl.loop(0, HERE)
        def _(other):
            pl.semaphore_signal(
                barrier,
                inc=1,
                device_id=(tm - c + lax.rem(other, 2), (other // 2) * 2 + c),
                device_id_type=MESH,
            )

    @pl.loop(1, HERE)
    def _(d):
        pl.semaphore_signal(
            barrier, inc=1, device_id=in_plane(lax.rem(q + d, HERE)), device_id_type=MESH
        )

    @pl.loop(1, SLICES)
    def _(d):
        pl.semaphore_signal(
            barrier, inc=1, device_id=worker(lax.rem(j + d, SLICES)), device_id_type=MESH
        )

    home_nbr[...] = jnp.zeros_like(home_nbr)
    home_nbr[:, 0:NB] = neighbours_ref[...]
    pl.semaphore_wait(barrier, SLICES - 1 + HERE - 1 + HERE // 2)

    def remote(src, dst, send, recv, device):
        return pltpu.make_async_remote_copy(
            src_ref=src, dst_ref=dst, send_sem=send, recv_sem=recv,
            device_id=device, device_id_type=MESH,
        )

    def arrived(ref, sem):
        pltpu.make_async_copy(ref, ref, sem).wait()

    @pl.when(keeps)
    def _():
        pltpu.make_async_copy(home_nbr, nbr, nbr_sem).start()

    def field(i):
        return remote(
            forcing_ref.at[i], fields.at[i], swap_send.at[i], field_sem.at[i], partner
        )

    fetched = pl.ds(2 * x, 2)
    opposite = pl.ds(2 * lax.rem(x + 2, 4), 2)

    @pl.when(moves)
    def _():
        remote(home_nbr, nbr, swap_send.at[5], nbr_sem, partner).start()
        remote(
            blocks_ref.at[fetched], weights.at[fetched], swap_send.at[4], weight_sem, partner
        ).start()
        arrived(weights.at[pl.ds(0, 2)], swap_send.at[4])
        remote(
            blocks_ref.at[opposite], weights.at[opposite], swap_send.at[7], far_sem, partner
        ).start()

    @pl.when((tm == 0) & (zh == 1))
    def _():
        remote(init_ref, start, swap_send.at[6], start_sem, partner).start()

    @pl.when((tm == 0) & (zh == 0))
    def _():
        pltpu.make_async_copy(init_ref, start, start_sem).start()

    modes = modes_ref[...]
    wide = jnp.concatenate([jnp.concatenate([modes] * 4, axis=1)] * 4, axis=0)
    row = lax.broadcasted_iota(jnp.int32, (4 * Q, HALF), 0)
    col = lax.broadcasted_iota(jnp.int32, (4 * Q, HALF), 1)
    wide = jnp.where(row // Q == col // BRICK, wide, 0.0)
    wide_high = wide.astype(BF16)
    wide_low = (wide - wide_high.astype(F32)).astype(BF16)
    restrict[...] = jnp.concatenate([wide_high, wide_low, wide_high], axis=1)
    prolong[...] = jnp.concatenate(
        [wide_high.astype(F32), wide_low.astype(F32)], axis=0
    ).T.astype(BF16)

    def restricted(values):
        high_part = values.astype(BF16)
        low_part = (values - high_part.astype(F32)).astype(BF16)
        return dot(restrict[...], jnp.concatenate([high_part, high_part, low_part], axis=0))

    def prolonged(rounded):
        return dot(prolong[...], jnp.concatenate([rounded, rounded], axis=0))


    owns = keeps & (zl < 2)
    group = lax.rem(zl, 2)
    @pl.when(owns)
    def _():
        four = coarse_ref[pl.ds(4 * group, 4)].reshape(4 * Q, Q)
        row = lax.broadcasted_iota(jnp.int32, (4 * Q, 4 * Q), 0)
        col = lax.broadcasted_iota(jnp.int32, (4 * Q, 4 * Q), 1)
        power = jnp.where(row // Q == col // Q, jnp.concatenate([four] * 4, axis=1), 0.0)
        chain = (row == col).astype(F32)
        while chain.shape[1] < SLICES * 4 * Q:
            chain = jnp.concatenate([dot32(power, chain), chain], axis=1)
            power = dot32(power, power)
        strip[:, 0 : SLICES * 4 * Q] = chain
        strip[:, SLICES * 4 * Q :] = jnp.zeros((4 * Q, SLICES * 4 * Q), F32)
        near = strip[:, pl.ds(pl.multiple_of((3 - x) * 256, 256), 1280)]
        for d in range(9):
            first = (8 - d) * 4 * Q
            part = near[:, first : first + SLICES * 4 * Q]
            high_part = part.astype(BF16)
            toep_high[d * 4 * Q : (d + 1) * 4 * Q, :] = high_part
            toep_low[d * 4 * Q : (d + 1) * 4 * Q, :] = (part - high_part.astype(F32)).astype(BF16)

    tall = jnp.concatenate([modes] * 16, axis=0).T
    row = lax.broadcasted_iota(jnp.int32, (BRICK, ENS), 0) * 0 + 8 * c
    col = lax.broadcasted_iota(jnp.int32, (BRICK, ENS), 1) // Q
    for b in range(HERE):
        columns[b * BRICK : (b + 1) * BRICK, :] = jnp.where(
            (row + b == col) & (y == x), tall, 0.0
        )

    arrived(nbr, nbr_sem)

    @pl.when(keeps)
    def _():
        arrived(weights, weight_sem)

    @pl.when(moves)
    def _():
        arrived(weights.at[pl.ds(0, 2)], weight_sem)
        for d in (1, 3):
            remote(
                weights.at[fetched], weights.at[fetched], row_send, row_recv,
                (lax.rem(x + d, 4) * 8 + zl * 2 + c, sp),
            ).start()
        field(0).start()
        field(1).start()
        arrived(weights.at[pl.ds(0, 2)], far_sem)
        arrived(weights.at[pl.ds(0, 4)], row_recv)

    brick_ids = lax.broadcasted_iota(jnp.int32, (HERE, 128), 0)
    shift = lax.rem(nbr[...] - (8 * q + brick_ids) + (REACH + 64), 64)
    window = shift + lax.rem(brick_ids, 4)
    nbr[...] = jnp.where(brick_ids < 4, lax.rem(window + 8, 12), window)
    lane_brick = lax.broadcasted_iota(jnp.int32, (BRICK, 128), 1) // BRICK

    @pl.loop(0, HERE)
    def _(b):
        g, b4 = b // 4, lax.rem(b, 4)
        rows = pl.ds(pl.multiple_of(b4 * BRICK, BRICK), BRICK)
        places = nbr[pl.ds(b, 1), :]
        where = [jnp.broadcast_to(places[:, k : k + 1], (BRICK, 128)) for k in range(NB)]
        twice = []
        for k in range(NB + 1):
            block = weights[b, :, k * BRICK : (k + 1) * BRICK].astype(F32)
            twice.append(jnp.concatenate([block, block], axis=1))
        for pair in range(6):
            there = lane_brick + 2 * pair
            block = jnp.zeros((BRICK, 128), F32)
            for k in range(NB):
                block = jnp.where(where[k] == there, twice[k + 1], block)
            band[g, rows, pair * 128 : (pair + 1) * 128] = block.astype(BF16)
        for pair in range(2):
            block = jnp.where(lane_brick + 2 * pair == b4, twice[0], 0.0)
            diag[g, rows, pair * 128 : (pair + 1) * 128] = block.astype(BF16)

    exts = ((ext00, ext01), (ext10, ext11))

    def rows_of(g):
        return pl.ds(pl.multiple_of(g * HALF, HALF), HALF)

    def halo(u, sweep, g):
        ext = exts[u][sweep]
        return remote(
            ext.at[rows_of(g)], ext.at[rows_of(3 - g)],
            halo_send.at[u, sweep, g], halo_recv.at[u, sweep, 1 - g],
            in_plane(lax.rem(q + 7 + 2 * g, HERE)),
        )

    def solved(g, values):
        return dot(diag[g], values.astype(BF16))

    def send_half(u, sweep, g, values):
        exts[u][sweep][rows_of(g), :] = values.astype(BF16)
        halo(u, sweep, g).start()

    def swept(u, sweep, g):
        ext = exts[u][sweep]
        near = dot(band[g, :, : 2 * HALF], ext[0 : 2 * HALF, :])
        inner = solved(g, (state, columns)[u][rows_of(g), :] - near)
        arrived(ext.at[rows_of(2 + g)], halo_recv.at[u, sweep, g])
        return inner - dot(folded[g], ext[rows_of(2 + g), :])

    def halves(g):
        return slice(g * HALF, (g + 1) * HALF)

    def share(i):
        for d in range(1, 4):
            remote(
                powers.at[i, x], powers.at[i, x], power_send.at[i], power_recv.at[i],
                (lax.rem(x + d, 4) * 8 + zl * 2 + c, sp),
            ).start()

    def forward(i):
        arrived(powers.at[i, pl.ds(0, 3)], power_recv.at[i])
        pltpu.make_async_copy(powers.at[i], home_powers.at[i], home_power_sem.at[i]).start()
        remote(
            powers.at[i], home_powers.at[i], forward_send.at[i], home_power_sem.at[i],
            (tm - c + (1 - c), sp),
        ).start()

    def bring(source, target, send, recv):
        @pl.when(keeps)
        def _():
            pltpu.make_async_copy(source, target, recv).start()

        @pl.when(moves)
        def _():
            remote(source, target, send, recv, partner).start()

    @pl.when(j == 0)
    def _():
        arrived(start, start_sem)
        state[...] = start[...]

    @pl.when(j != 0)
    def _():
        state[...] = jnp.zeros_like(state)

    for u, ref in enumerate((state, columns)):
        for g in (slow, fast):
            send_half(u, 0, g, solved(g, ref[rows_of(g), :]))
    for g in range(2):
        folded[g] = dot(diag[g], band[g, :, 2 * HALF :]).astype(BF16)

    @pl.loop(0, STEPS)
    def _(i):
        @pl.when(moves & (i < 2))
        def _():
            field(i + 2).start()

        for g in (fast, slow):
            for u in range(2):
                send_half(u, 1, g, swept(u, 0, g))
        arrived(fields.at[i], field_sem.at[i])
        for g in (fast, slow):
            for u in range(2):
                following = swept(u, 1, g)
                arrived(ext00.at[rows_of(0)], halo_send.at[u, 0, g])
                arrived(ext00.at[rows_of(0)], halo_send.at[u, 1, g])
                if u == 0:
                    following += fields[i, rows_of(g), :].astype(F32)
                    state[rows_of(g), :] = following
                    held[i, rows_of(g), :] = following.astype(BF16)
                else:
                    columns[rows_of(g), :] = following
                    powers[i, x, rows_of(g), :] = following.astype(BF16)

                @pl.when(i < STEPS - 1)
                def _():
                    send_half(u, 0, g, solved(g, following))

        @pl.when(i < STEPS - 1)
        def _():
            bring(held.at[i], home_held.at[i], held_send.at[i], home_held_sem.at[i])

        @pl.when((i < STEPS - 1) & keeps)
        def _():
            share(i)

        @pl.when((i > 0) & keeps)
        def _():
            forward(i - 1)

    def coarse_part(ref, i, gathered, g):
        matrix = jnp.concatenate([ref[i, n, halves(g), :] for n in range(4)], axis=1)
        return dot(matrix, gathered[...])

    sum_prev = sum_here = None
    for it, (incoming, err, got, gathered) in enumerate(
        ((in0, err0, got0, all0), (in1, err1, got1, all1))
    ):
        for g in range(2):
            defect = state[halves(g), :]
            if it:
                defect += coarse_part(powers, STEPS - 1, all0, g)
                defect -= prolonged(got0[g, 1])
                stage[STEPS, halves(g), :] = defect.astype(BF16)
            r_buf[it, g] = restricted(defect).astype(BF16)

        @pl.loop(0, 8)
        def _(w):
            g = lax.rem(w, 2)
            owner_tm = (w // 2) * 8 + g * 2 + c
            owner_sp = 2 * y + c
            mine = (owner_tm == tm) & (owner_sp == sp)

            @pl.when(mine)
            def _():
                incoming[j] = r_buf[it, g]

            @pl.when(jnp.logical_not(mine))
            def _():
                remote(
                    r_buf.at[it, g], incoming.at[j], sc_send.at[it, 0], sc_recv.at[it, 0],
                    (owner_tm, owner_sp),
                ).start()

        if it:
            bring(stage.at[STEPS], def_ref, out_send, def_recv)
        else:
            share(STEPS - 1)

        @pl.when(owns)
        def _():
            arrived(incoming.at[pl.ds(0, SLICES - 1)], sc_recv.at[it, 0])
            terms = incoming[...].reshape(SLICES * 4 * Q, ENS)
            errors = dot(toep_high[...], terms) + dot(toep_low[...], terms)
            err[...] = errors.astype(BF16).reshape(9, 4 * Q, ENS)

            @pl.loop(0, 8)
            def _(d):
                there = x * 8 + d

                @pl.when(there == j)
                def _():
                    got[group] = err[pl.ds(d, 2)]

                @pl.when(there != j)
                def _():
                    remote(
                        err.at[pl.ds(d, 2)], got.at[group],
                        sc_send.at[it, 1], sc_recv.at[it, 1], worker(there),
                    ).start()

            arrived(got.at[0], sc_recv.at[it, 1])

        @pl.when(jnp.logical_not(owns))
        def _():
            arrived(got, sc_recv.at[it, 1])

        e_prev = [got[g, 0].astype(F32) for g in range(2)]
        e_here = [got[g, 1].astype(F32) for g in range(2)]
        if it:
            e_prev = [a + b for a, b in zip(e_prev, sum_prev)]
            e_here = [a + b for a, b in zip(e_here, sum_here)]
        sum_prev, sum_here = e_prev, e_here
        mine = pl.ds(pl.multiple_of(q * HERE * Q, HERE * Q), HERE * Q)
        rounded_prev = jnp.concatenate(sum_prev, axis=0).astype(BF16)
        if it == 0:
            gathered[mine, :] = rounded_prev

            @pl.loop(1, HERE)
            def _(d):
                remote(
                    gathered.at[mine], gathered.at[mine], all_send.at[it], all_recv.at[it],
                    in_plane(lax.rem(q + d, HERE)),
                ).start()

            arrived(powers.at[STEPS - 1, pl.ds(0, 3)], power_recv.at[STEPS - 1])
            arrived(gathered.at[pl.ds(0, 7 * HERE * Q)], all_recv.at[it])
        else:
            prev_buf[...] = rounded_prev
            here_buf[...] = jnp.concatenate(sum_here, axis=0).astype(BF16)

            @pl.loop(0, HERE)
            def _(d):
                home = lax.rem(sp + d, HERE)
                own = keeps & (home == sp)

                @pl.when(own)
                def _():
                    gathered[mine, :] = prev_buf[...]

                @pl.when(jnp.logical_not(own))
                def _():
                    remote(
                        prev_buf, gathered.at[mine], all_send.at[it], all_recv.at[it],
                        (tm - c + zh, home),
                    ).start()

            bring(here_buf, home_here, here_send, here_recv)

    @pl.when(keeps)
    def _():
        arrived(all1.at[pl.ds(0, 7 * HERE * Q)], all_recv.at[1])

    @pl.when(moves)
    def _():
        arrived(all1, all_recv.at[1])

    for i in range(STEPS - 1):
        arrived(home_held.at[i], home_held_sem.at[i])
        arrived(home_powers.at[i], home_power_sem.at[i])
        for g in range(2):
            value = home_held[i, halves(g), :].astype(F32) + coarse_part(home_powers, i, all1, g)
            stage[i, halves(g), :] = value.astype(BF16)
        pltpu.make_async_copy(stage.at[i], sol_ref.at[i], sol_recv).start()
    arrived(home_here, here_recv)
    for g in range(2):
        part = home_here[g * 4 * Q : (g + 1) * 4 * Q, :]
        stage[STEPS - 1, halves(g), :] = prolonged(part).astype(BF16)
    pltpu.make_async_copy(stage.at[STEPS - 1], sol_ref.at[STEPS - 1], sol_recv).start()

    for it, incoming in enumerate((in0, in1)):

        @pl.when(owns)
        def _():
            arrived(incoming.at[pl.ds(0, 7)], sc_send.at[it, 0])
            arrived(incoming.at[pl.ds(0, 14)], sc_send.at[it, 1])

        @pl.when(jnp.logical_not(owns))
        def _():
            arrived(incoming.at[pl.ds(0, 8)], sc_send.at[it, 0])

    arrived(all0.at[pl.ds(0, 7 * HERE * Q)], all_send.at[0])
    arrived(powers.at[STEPS - 1, pl.ds(0, 3)], power_send.at[STEPS - 1])

    @pl.when(keeps)
    def _():
        arrived(all0.at[pl.ds(0, 7 * HERE * Q)], all_send.at[1])
        for i in range(STEPS - 1):
            arrived(powers.at[i, pl.ds(0, 3)], power_send.at[i])
            arrived(powers.at[i], forward_send.at[i])

    @pl.when(moves)
    def _():
        arrived(all0, all_send.at[1])
        arrived(home_nbr, swap_send.at[5])
        arrived(weights.at[pl.ds(0, 2)], swap_send.at[7])
        arrived(weights.at[pl.ds(0, 4)], row_send)
        for i in range(STEPS):
            arrived(fields.at[i], swap_send.at[i])
        for i in range(STEPS - 1):
            arrived(held.at[i], held_send.at[i])
        arrived(stage.at[STEPS], out_send)
        arrived(here_buf, here_send)

    @pl.when((tm == 0) & (zh == 1))
    def _():
        arrived(start, swap_send.at[6])

    arrived(sol_ref, sol_recv)
    arrived(def_ref, def_recv)


def body(initial, forcing, brick_blocks, neighbours, coarse_modes, coarse_blocks):
    vmem = pl.BlockSpec(memory_space=pltpu.VMEM)
    hbm = pl.BlockSpec(memory_space=pl.ANY)
    sem = pltpu.SemaphoreType.DMA
    sol, last = pl.pallas_call(
        kernel,
        out_shape=(
            jax.ShapeDtypeStruct((STEPS, ROWS, ENS), BF16),
            jax.ShapeDtypeStruct((ROWS, ENS), BF16),
        ),
        in_specs=[hbm, hbm, hbm, vmem, vmem, vmem],
        out_specs=(hbm, hbm),
        scratch_shapes=[
            pltpu.VMEM((STEPS, ROWS, ENS), BF16),
            pltpu.VMEM((HERE, BRICK, (NB + 1) * BRICK), BF16),
            pltpu.VMEM((HERE, 128), jnp.int32),
            pltpu.VMEM((HERE, 128), jnp.int32),
            pltpu.VMEM((ROWS, ENS), F32),
            pltpu.VMEM((ROWS, ENS), F32),
            pltpu.VMEM((ROWS, ENS), F32),
            pltpu.VMEM((2, HALF, 3 * HALF), BF16),
            pltpu.VMEM((2, HALF, HALF), BF16),
            pltpu.VMEM((2, HALF, HALF), BF16),
            *[pltpu.VMEM((4 * HALF, ENS), BF16)] * 4,
            pltpu.VMEM((4 * Q, 3 * HALF), BF16),
            pltpu.VMEM((HALF, 8 * Q), BF16),
            pltpu.VMEM((4 * Q, 2 * SLICES * 4 * Q), F32),
            pltpu.VMEM((9 * 4 * Q, SLICES * 4 * Q), BF16),
            pltpu.VMEM((9 * 4 * Q, SLICES * 4 * Q), BF16),
            pltpu.VMEM((ITERS, 2, 4 * Q, ENS), BF16),
            *[pltpu.VMEM((SLICES, 4 * Q, ENS), BF16)] * 2,
            *[pltpu.VMEM((9, 4 * Q, ENS), BF16)] * 2,
            *[pltpu.VMEM((2, 2, 4 * Q, ENS), BF16)] * 2,
            *[pltpu.VMEM((HERE * HERE * Q, ENS), BF16)] * 2,
            pltpu.VMEM((STEPS, 4, ROWS, ENS), BF16),
            pltpu.VMEM((STEPS - 1, 4, ROWS, ENS), BF16),
            pltpu.VMEM((STEPS, ROWS, ENS), BF16),
            pltpu.VMEM((STEPS - 1, ROWS, ENS), BF16),
            *[pltpu.VMEM((HERE * Q, ENS), BF16)] * 3,
            pltpu.VMEM((STEPS + 1, ROWS, ENS), BF16),
            sem((STEPS,)),
            sem,
            sem,
            sem,
            sem,
            sem((2, 2, 2)),
            sem((2, 2, 2)),
            sem((8,)),
            sem,
            sem,
            sem((ITERS, 2)),
            sem((ITERS, 2)),
            sem((ITERS,)),
            sem((ITERS,)),
            sem((STEPS,)),
            sem((STEPS,)),
            sem((STEPS - 1,)),
            sem((STEPS - 1,)),
            sem((STEPS - 1,)),
            sem((STEPS - 1,)),
            sem,
            sem,
            sem,
            sem,
            sem,
        ],
        compiler_params=pltpu.CompilerParams(
            collective_id=0, has_side_effects=True, vmem_limit_bytes=60 * 2**20
        ),
    )(
        initial.reshape(ROWS, ENS),
        forcing.reshape(STEPS, ROWS, ENS),
        brick_blocks,
        neighbours,
        coarse_modes,
        coarse_blocks,
    )
    return (
        sol.astype(F32).reshape(STEPS, HERE, BRICK, ENS),
        last.astype(F32).reshape(1, HERE, BRICK, ENS),
    )


def solution(mesh):
    placed = (
        P("space", None, None),
        P("tm", "space", None, None),
        P("space", None, None),
        P("space", None),
        P(),
        P("space", None, None),
    )
    return jax.shard_map(
        body,
        mesh=mesh,
        in_specs=placed,
        out_specs=(P("tm", "space", None, None), P("tm", "space", None, None)),
        check_vma=False,
    )
```

```python
import functools

import jax
import jax.numpy as jnp
from jax import lax
from jax.experimental import pallas as pl
from jax.experimental.pallas import tpu as pltpu
from jax.sharding import PartitionSpec as P

BRICK = 64
ENS = 128
NB = 6
REACH = 4
Q = 8
STEPS = 4
ITERS = 2
HERE = 8
SLICES = 32
ROWS = HERE * BRICK
HALF = ROWS // 2

MESH = pl.DeviceIdType.MESH
HIGHEST = lax.Precision.HIGHEST
F32 = jnp.float32
BF16 = jnp.bfloat16


def dot(a, b):
    return jnp.dot(a, b, preferred_element_type=F32)


def dot32(a, b):
    return jnp.dot(a, b, preferred_element_type=F32, precision=HIGHEST)


def kernel(
    init_ref, forcing_ref, blocks_ref, neighbours_ref, modes_ref, coarse_ref,
    sol_ref, def_ref,
    fields, weights, home_nbr, nbr, start, state, columns, band, folded, diag, ext00, ext01, ext10, ext11,
    restrict, prolong, coarse_map, strip, toep_high, toep_low, r_buf, in0, in1, err0, err1, got0, got1, all0, all1,
    powers, home_powers, held, home_held, prev_buf, here_buf, home_here, stage,
    field_sem, weight_sem, far_sem, nbr_sem, start_sem, halo_send, halo_recv, swap_send, row_send, row_recv,
    sc_send, sc_recv, all_send, all_recv, power_send, power_recv, forward_send, home_power_sem,
    held_send, home_held_sem, here_send, here_recv, out_send, sol_recv, def_recv,
):
    tm = lax.axis_index("tm")
    sp = lax.axis_index("space")
    c = lax.rem(tm, 2)
    zl = lax.rem(tm // 2, 4)
    x = tm // 8
    y = sp // 2
    zh = lax.rem(sp, 2)
    keeps = c == zh
    moves = c != zh
    j = x * 8 + zl * 2 + zh
    q = 2 * y + c
    partner = (tm - c + zh, sp - zh + c)
    slow, fast = c, 1 - c

    def worker(slice_id):
        return (
            (slice_id // 8) * 8 + lax.rem(slice_id // 2, 4) * 2 + c,
            2 * y + lax.rem(slice_id, 2),
        )

    def in_plane(other):
        return (tm - c + lax.rem(other, 2), (other // 2) * 2 + zh)

    @pl.when(keeps)
    def _():
        pltpu.make_async_copy(blocks_ref, weights, weight_sem).start()
        for i in range(STEPS):
            pltpu.make_async_copy(forcing_ref.at[i], fields.at[i], field_sem.at[i]).start()

    barrier = pltpu.get_barrier_semaphore()

    @pl.when(moves)
    def _():
        @pl.loop(0, HERE)
        def _(other):
            pl.semaphore_signal(
                barrier,
                inc=1,
                device_id=(tm - c + lax.rem(other, 2), (other // 2) * 2 + c),
                device_id_type=MESH,
            )

    @pl.loop(1, HERE)
    def _(d):
        pl.semaphore_signal(
            barrier, inc=1, device_id=in_plane(lax.rem(q + d, HERE)), device_id_type=MESH
        )

    @pl.loop(1, SLICES)
    def _(d):
        pl.semaphore_signal(
            barrier, inc=1, device_id=worker(lax.rem(j + d, SLICES)), device_id_type=MESH
        )

    home_nbr[...] = jnp.zeros_like(home_nbr)
    home_nbr[:, 0:NB] = neighbours_ref[...]
    pl.semaphore_wait(barrier, SLICES - 1 + HERE - 1 + HERE // 2)

    def remote(src, dst, send, recv, device):
        return pltpu.make_async_remote_copy(
            src_ref=src, dst_ref=dst, send_sem=send, recv_sem=recv,
            device_id=device, device_id_type=MESH,
        )

    def arrived(ref, sem):
        pltpu.make_async_copy(ref, ref, sem).wait()

    @pl.when(keeps)
    def _():
        pltpu.make_async_copy(home_nbr, nbr, nbr_sem).start()

    def field(i):
        return remote(
            forcing_ref.at[i], fields.at[i], swap_send.at[i], field_sem.at[i], partner
        )

    fetched = pl.ds(2 * x, 2)
    opposite = pl.ds(2 * lax.rem(x + 2, 4), 2)

    @pl.when(moves)
    def _():
        remote(home_nbr, nbr, swap_send.at[5], nbr_sem, partner).start()
        remote(
            blocks_ref.at[fetched], weights.at[fetched], swap_send.at[4], weight_sem, partner
        ).start()
        arrived(weights.at[pl.ds(0, 2)], swap_send.at[4])
        remote(
            blocks_ref.at[opposite], weights.at[opposite], swap_send.at[7], far_sem, partner
        ).start()

    @pl.when((tm == 0) & (zh == 1))
    def _():
        remote(init_ref, start, swap_send.at[6], start_sem, partner).start()

    @pl.when((tm == 0) & (zh == 0))
    def _():
        pltpu.make_async_copy(init_ref, start, start_sem).start()

    modes = modes_ref[...]
    wide = jnp.concatenate([jnp.concatenate([modes] * 4, axis=1)] * 4, axis=0)
    row = lax.broadcasted_iota(jnp.int32, (4 * Q, HALF), 0)
    col = lax.broadcasted_iota(jnp.int32, (4 * Q, HALF), 1)
    wide = jnp.where(row // Q == col // BRICK, wide, 0.0)
    wide_high = wide.astype(BF16)
    wide_low = (wide - wide_high.astype(F32)).astype(BF16)
    restrict[...] = jnp.concatenate([wide_high, wide_low, wide_high], axis=1)
    prolong[...] = jnp.concatenate(
        [wide_high.astype(F32), wide_low.astype(F32)], axis=0
    ).T.astype(BF16)

    def restricted(values):
        high_part = values.astype(BF16)
        low_part = (values - high_part.astype(F32)).astype(BF16)
        return dot(restrict[...], jnp.concatenate([high_part, high_part, low_part], axis=0))

    def prolonged(rounded):
        return dot(prolong[...], jnp.concatenate([rounded, rounded], axis=0))


    owns = keeps & (zl < 2)
    group = lax.rem(zl, 2)
    @pl.when(owns)
    def _():
        four = coarse_ref[pl.ds(4 * group, 4)].reshape(4 * Q, Q)
        row = lax.broadcasted_iota(jnp.int32, (4 * Q, 4 * Q), 0)
        col = lax.broadcasted_iota(jnp.int32, (4 * Q, 4 * Q), 1)
        power = jnp.where(row // Q == col // Q, jnp.concatenate([four] * 4, axis=1), 0.0)
        chain = (row == col).astype(F32)
        while chain.shape[1] < SLICES * 4 * Q:
            chain = jnp.concatenate([dot32(power, chain), chain], axis=1)
            power = dot32(power, power)
        strip[:, 0 : SLICES * 4 * Q] = chain
        strip[:, SLICES * 4 * Q :] = jnp.zeros((4 * Q, SLICES * 4 * Q), F32)
        near = strip[:, pl.ds(pl.multiple_of((3 - x) * 256, 256), 1280)]
        for d in range(9):
            first = (8 - d) * 4 * Q
            part = near[:, first : first + SLICES * 4 * Q]
            high_part = part.astype(BF16)
            toep_high[d * 4 * Q : (d + 1) * 4 * Q, :] = high_part
            toep_low[d * 4 * Q : (d + 1) * 4 * Q, :] = (part - high_part.astype(F32)).astype(BF16)

    tall = jnp.concatenate([modes] * 16, axis=0).T
    row = lax.broadcasted_iota(jnp.int32, (BRICK, ENS), 0) * 0 + 8 * c
    col = lax.broadcasted_iota(jnp.int32, (BRICK, ENS), 1) // Q
    for b in range(HERE):
        columns[b * BRICK : (b + 1) * BRICK, :] = jnp.where(
            (row + b == col) & (y == x), tall, 0.0
        )

    arrived(nbr, nbr_sem)

    @pl.when(keeps)
    def _():
        arrived(weights, weight_sem)

    @pl.when(moves)
    def _():
        arrived(weights.at[pl.ds(0, 2)], weight_sem)
        for d in (1, 3):
            remote(
                weights.at[fetched], weights.at[fetched], row_send, row_recv,
                (lax.rem(x + d, 4) * 8 + zl * 2 + c, sp),
            ).start()
        field(0).start()
        field(1).start()
        arrived(weights.at[pl.ds(0, 2)], far_sem)
        arrived(weights.at[pl.ds(0, 4)], row_recv)

    brick_ids = lax.broadcasted_iota(jnp.int32, (HERE, 128), 0)
    shift = lax.rem(nbr[...] - (8 * q + brick_ids) + (REACH + 64), 64)
    window = shift + lax.rem(brick_ids, 4)
    nbr[...] = jnp.where(brick_ids < 4, lax.rem(window + 8, 12), window)
    lane_brick = lax.broadcasted_iota(jnp.int32, (BRICK, 128), 1) // BRICK

    @pl.loop(0, HERE)
    def _(b):
        g, b4 = b // 4, lax.rem(b, 4)
        rows = pl.ds(pl.multiple_of(b4 * BRICK, BRICK), BRICK)
        places = nbr[pl.ds(b, 1), :]
        where = [jnp.broadcast_to(places[:, k : k + 1], (BRICK, 128)) for k in range(NB)]
        twice = []
        for k in range(NB + 1):
            block = weights[b, :, k * BRICK : (k + 1) * BRICK].astype(F32)
            twice.append(jnp.concatenate([block, block], axis=1))
        for pair in range(6):
            there = lane_brick + 2 * pair
            block = jnp.zeros((BRICK, 128), F32)
            for k in range(NB):
                block = jnp.where(where[k] == there, twice[k + 1], block)
            band[g, rows, pair * 128 : (pair + 1) * 128] = block.astype(BF16)
        for pair in range(2):
            block = jnp.where(lane_brick + 2 * pair == b4, twice[0], 0.0)
            diag[g, rows, pair * 128 : (pair + 1) * 128] = block.astype(BF16)

    exts = ((ext00, ext01), (ext10, ext11))

    def rows_of(g):
        return pl.ds(pl.multiple_of(g * HALF, HALF), HALF)

    def halo(u, sweep, g):
        ext = exts[u][sweep]
        return remote(
            ext.at[rows_of(g)], ext.at[rows_of(3 - g)],
            halo_send.at[u, sweep, g], halo_recv.at[u, sweep, 1 - g],
            in_plane(lax.rem(q + 7 + 2 * g, HERE)),
        )

    def solved(g, values):
        return dot(diag[g], values.astype(BF16))

    def send_half(u, sweep, g, values):
        exts[u][sweep][rows_of(g), :] = values.astype(BF16)
        halo(u, sweep, g).start()

    def swept(u, sweep, g):
        ext = exts[u][sweep]
        near = dot(band[g, :, : 2 * HALF], ext[0 : 2 * HALF, :])
        inner = solved(g, (state, columns)[u][rows_of(g), :] - near)
        arrived(ext.at[rows_of(2 + g)], halo_recv.at[u, sweep, g])
        return inner - dot(folded[g], ext[rows_of(2 + g), :])

    def halves(g):
        return slice(g * HALF, (g + 1) * HALF)

    def share(i):
        for d in range(1, 4):
            remote(
                powers.at[i, x], powers.at[i, x], power_send.at[i], power_recv.at[i],
                (lax.rem(x + d, 4) * 8 + zl * 2 + c, sp),
            ).start()

    def forward(i):
        arrived(powers.at[i, pl.ds(0, 3)], power_recv.at[i])
        pltpu.make_async_copy(powers.at[i], home_powers.at[i], home_power_sem.at[i]).start()
        remote(
            powers.at[i], home_powers.at[i], forward_send.at[i], home_power_sem.at[i],
            (tm - c + (1 - c), sp),
        ).start()

    def bring(source, target, send, recv):
        @pl.when(keeps)
        def _():
            pltpu.make_async_copy(source, target, recv).start()

        @pl.when(moves)
        def _():
            remote(source, target, send, recv, partner).start()

    @pl.when(j == 0)
    def _():
        arrived(start, start_sem)
        state[...] = start[...]

    @pl.when(j != 0)
    def _():
        state[...] = jnp.zeros_like(state)

    def to_owners(it, incoming):
        @pl.loop(0, 8)
        def _(w):
            g = lax.rem(w, 2)
            owner_tm = (w // 2) * 8 + g * 2 + c
            owner_sp = 2 * y + c
            mine = (owner_tm == tm) & (owner_sp == sp)

            @pl.when(mine)
            def _():
                incoming[j] = r_buf[it, g]

            @pl.when(jnp.logical_not(mine))
            def _():
                remote(
                    r_buf.at[it, g], incoming.at[j], sc_send.at[it, 0], sc_recv.at[it, 0],
                    (owner_tm, owner_sp),
                ).start()

    for u, ref in enumerate((state, columns)):
        for g in (slow, fast):
            send_half(u, 0, g, solved(g, ref[rows_of(g), :]))
    for g in range(2):
        folded[g] = dot(diag[g], band[g, :, 2 * HALF :]).astype(BF16)

    @pl.loop(0, STEPS)
    def _(i):
        @pl.when(moves & (i < 2))
        def _():
            field(i + 2).start()

        for g in (fast, slow):
            for u in range(2):
                send_half(u, 1, g, swept(u, 0, g))
        arrived(fields.at[i], field_sem.at[i])
        for g, u in ((fast, 0), (fast, 1), (slow, 0), (slow, 1)):
            following = swept(u, 1, g)
            arrived(ext00.at[rows_of(0)], halo_send.at[u, 0, g])
            arrived(ext00.at[rows_of(0)], halo_send.at[u, 1, g])
            if u == 0:
                following += fields[i, rows_of(g), :].astype(F32)
                state[rows_of(g), :] = following

                @pl.when(i == STEPS - 1)
                def _():
                    r_buf[0, g] = restricted(following).astype(BF16)
                    if g is slow:
                        to_owners(0, in0)

                held[i, rows_of(g), :] = following.astype(BF16)
            else:
                columns[rows_of(g), :] = following
                powers[i, x, rows_of(g), :] = following.astype(BF16)

            @pl.when(i < STEPS - 1)
            def _():
                send_half(u, 0, g, solved(g, following))

        @pl.when(i < STEPS - 1)
        def _():
            bring(held.at[i], home_held.at[i], held_send.at[i], home_held_sem.at[i])

        @pl.when((i < STEPS - 1) & keeps)
        def _():
            share(i)

        @pl.when((i > 0) & keeps)
        def _():
            forward(i - 1)

    def coarse_part(ref, i, gathered, g):
        matrix = jnp.concatenate([ref[i, n, halves(g), :] for n in range(4)], axis=1)
        return dot(matrix, gathered[...])

    sum_prev = sum_here = None
    for it, (incoming, err, got, gathered) in enumerate(
        ((in0, err0, got0, all0), (in1, err1, got1, all1))
    ):
        if it:
            for g in range(2):
                r_buf[1, g] = (known[g] + dot(coarse_map[g], all0[...])).astype(BF16)
            to_owners(1, in1)
            for g in range(2):
                defect = state[halves(g), :] + coarse_part(powers, STEPS - 1, all0, g)
                stage[STEPS, halves(g), :] = (defect - prolonged(got0[g, 1])).astype(BF16)

        if it:
            bring(stage.at[STEPS], def_ref, out_send, def_recv)
        else:
            share(STEPS - 1)

        @pl.when(owns)
        def _():
            arrived(incoming.at[pl.ds(0, SLICES - 1)], sc_recv.at[it, 0])
            terms = incoming[...].reshape(SLICES * 4 * Q, ENS)
            errors = dot(toep_high[...], terms) + dot(toep_low[...], terms)
            err[...] = errors.astype(BF16).reshape(9, 4 * Q, ENS)

            @pl.loop(0, 8)
            def _(d):
                there = x * 8 + d

                @pl.when(there == j)
                def _():
                    got[group] = err[pl.ds(d, 2)]

                @pl.when(there != j)
                def _():
                    remote(
                        err.at[pl.ds(d, 2)], got.at[group],
                        sc_send.at[it, 1], sc_recv.at[it, 1], worker(there),
                    ).start()

            arrived(got.at[0], sc_recv.at[it, 1])

        @pl.when(jnp.logical_not(owns))
        def _():
            arrived(got, sc_recv.at[it, 1])

        e_prev = [got[g, 0].astype(F32) for g in range(2)]
        e_here = [got[g, 1].astype(F32) for g in range(2)]
        if it:
            e_prev = [a + b for a, b in zip(e_prev, sum_prev)]
            e_here = [a + b for a, b in zip(e_here, sum_here)]
        sum_prev, sum_here = e_prev, e_here
        mine = pl.ds(pl.multiple_of(q * HERE * Q, HERE * Q), HERE * Q)
        rounded_prev = jnp.concatenate(sum_prev, axis=0).astype(BF16)
        if it == 0:
            gathered[mine, :] = rounded_prev

            @pl.loop(1, HERE)
            def _(d):
                remote(
                    gathered.at[mine], gathered.at[mine], all_send.at[it], all_recv.at[it],
                    in_plane(lax.rem(q + d, HERE)),
                ).start()

            known = [restricted(state[halves(g), :] - prolonged(got[g, 1])) for g in range(2)]
            arrived(powers.at[STEPS - 1, pl.ds(0, 3)], power_recv.at[STEPS - 1])
            for g in range(2):
                last = [powers[STEPS - 1, n, halves(g), :] for n in range(4)]
                last = jnp.concatenate(last, axis=1)
                last = jnp.concatenate([last, last], axis=0)
                coarse_map[g] = dot(restrict[:, : 2 * HALF], last).astype(BF16)
            arrived(gathered.at[pl.ds(0, 7 * HERE * Q)], all_recv.at[it])
        else:
            prev_buf[...] = rounded_prev
            here_buf[...] = jnp.concatenate(sum_here, axis=0).astype(BF16)

            @pl.loop(0, HERE)
            def _(d):
                home = lax.rem(sp + d, HERE)
                own = keeps & (home == sp)

                @pl.when(own)
                def _():
                    gathered[mine, :] = prev_buf[...]

                @pl.when(jnp.logical_not(own))
                def _():
                    remote(
                        prev_buf, gathered.at[mine], all_send.at[it], all_recv.at[it],
                        (tm - c + zh, home),
                    ).start()

            bring(here_buf, home_here, here_send, here_recv)

    @pl.when(keeps)
    def _():
        arrived(all1.at[pl.ds(0, 7 * HERE * Q)], all_recv.at[1])

    @pl.when(moves)
    def _():
        arrived(all1, all_recv.at[1])

    for i in range(STEPS - 1):
        arrived(home_held.at[i], home_held_sem.at[i])
        arrived(home_powers.at[i], home_power_sem.at[i])
        for g in range(2):
            value = home_held[i, halves(g), :].astype(F32) + coarse_part(home_powers, i, all1, g)
            stage[i, halves(g), :] = value.astype(BF16)
        pltpu.make_async_copy(stage.at[i], sol_ref.at[i], sol_recv).start()
    arrived(home_here, here_recv)
    for g in range(2):
        part = home_here[g * 4 * Q : (g + 1) * 4 * Q, :]
        stage[STEPS - 1, halves(g), :] = prolonged(part).astype(BF16)
    pltpu.make_async_copy(stage.at[STEPS - 1], sol_ref.at[STEPS - 1], sol_recv).start()

    for it, incoming in enumerate((in0, in1)):

        @pl.when(owns)
        def _():
            arrived(incoming.at[pl.ds(0, 7)], sc_send.at[it, 0])
            arrived(incoming.at[pl.ds(0, 14)], sc_send.at[it, 1])

        @pl.when(jnp.logical_not(owns))
        def _():
            arrived(incoming.at[pl.ds(0, 8)], sc_send.at[it, 0])

    arrived(all0.at[pl.ds(0, 7 * HERE * Q)], all_send.at[0])
    arrived(powers.at[STEPS - 1, pl.ds(0, 3)], power_send.at[STEPS - 1])

    @pl.when(keeps)
    def _():
        arrived(all0.at[pl.ds(0, 7 * HERE * Q)], all_send.at[1])
        for i in range(STEPS - 1):
            arrived(powers.at[i, pl.ds(0, 3)], power_send.at[i])
            arrived(powers.at[i], forward_send.at[i])

    @pl.when(moves)
    def _():
        arrived(all0, all_send.at[1])
        arrived(home_nbr, swap_send.at[5])
        arrived(weights.at[pl.ds(0, 2)], swap_send.at[7])
        arrived(weights.at[pl.ds(0, 4)], row_send)
        for i in range(STEPS):
            arrived(fields.at[i], swap_send.at[i])
        for i in range(STEPS - 1):
            arrived(held.at[i], held_send.at[i])
        arrived(stage.at[STEPS], out_send)
        arrived(here_buf, here_send)

    @pl.when((tm == 0) & (zh == 1))
    def _():
        arrived(start, swap_send.at[6])

    arrived(sol_ref, sol_recv)
    arrived(def_ref, def_recv)


def body(initial, forcing, brick_blocks, neighbours, coarse_modes, coarse_blocks):
    vmem = pl.BlockSpec(memory_space=pltpu.VMEM)
    hbm = pl.BlockSpec(memory_space=pl.ANY)
    sem = pltpu.SemaphoreType.DMA
    sol, last = pl.pallas_call(
        kernel,
        out_shape=(
            jax.ShapeDtypeStruct((STEPS, ROWS, ENS), BF16),
            jax.ShapeDtypeStruct((ROWS, ENS), BF16),
        ),
        in_specs=[hbm, hbm, hbm, vmem, vmem, vmem],
        out_specs=(hbm, hbm),
        scratch_shapes=[
            pltpu.VMEM((STEPS, ROWS, ENS), BF16),
            pltpu.VMEM((HERE, BRICK, (NB + 1) * BRICK), BF16),
            pltpu.VMEM((HERE, 128), jnp.int32),
            pltpu.VMEM((HERE, 128), jnp.int32),
            pltpu.VMEM((ROWS, ENS), F32),
            pltpu.VMEM((ROWS, ENS), F32),
            pltpu.VMEM((ROWS, ENS), F32),
            pltpu.VMEM((2, HALF, 3 * HALF), BF16),
            pltpu.VMEM((2, HALF, HALF), BF16),
            pltpu.VMEM((2, HALF, HALF), BF16),
            *[pltpu.VMEM((4 * HALF, ENS), BF16)] * 4,
            pltpu.VMEM((4 * Q, 3 * HALF), BF16),
            pltpu.VMEM((HALF, 8 * Q), BF16),
            pltpu.VMEM((2, 4 * Q, HERE * HERE * Q), BF16),
            pltpu.VMEM((4 * Q, 2 * SLICES * 4 * Q), F32),
            pltpu.VMEM((9 * 4 * Q, SLICES * 4 * Q), BF16),
            pltpu.VMEM((9 * 4 * Q, SLICES * 4 * Q), BF16),
            pltpu.VMEM((ITERS, 2, 4 * Q, ENS), BF16),
            *[pltpu.VMEM((SLICES, 4 * Q, ENS), BF16)] * 2,
            *[pltpu.VMEM((9, 4 * Q, ENS), BF16)] * 2,
            *[pltpu.VMEM((2, 2, 4 * Q, ENS), BF16)] * 2,
            *[pltpu.VMEM((HERE * HERE * Q, ENS), BF16)] * 2,
            pltpu.VMEM((STEPS, 4, ROWS, ENS), BF16),
            pltpu.VMEM((STEPS - 1, 4, ROWS, ENS), BF16),
            pltpu.VMEM((STEPS, ROWS, ENS), BF16),
            pltpu.VMEM((STEPS - 1, ROWS, ENS), BF16),
            *[pltpu.VMEM((HERE * Q, ENS), BF16)] * 3,
            pltpu.VMEM((STEPS + 1, ROWS, ENS), BF16),
            sem((STEPS,)),
            sem,
            sem,
            sem,
            sem,
            sem((2, 2, 2)),
            sem((2, 2, 2)),
            sem((8,)),
            sem,
            sem,
            sem((ITERS, 2)),
            sem((ITERS, 2)),
            sem((ITERS,)),
            sem((ITERS,)),
            sem((STEPS,)),
            sem((STEPS,)),
            sem((STEPS - 1,)),
            sem((STEPS - 1,)),
            sem((STEPS - 1,)),
            sem((STEPS - 1,)),
            sem,
            sem,
            sem,
            sem,
            sem,
        ],
        compiler_params=pltpu.CompilerParams(
            collective_id=0, has_side_effects=True, vmem_limit_bytes=60 * 2**20
        ),
    )(
        initial.reshape(ROWS, ENS),
        forcing.reshape(STEPS, ROWS, ENS),
        brick_blocks,
        neighbours,
        coarse_modes,
        coarse_blocks,
    )
    return (
        sol.astype(F32).reshape(STEPS, HERE, BRICK, ENS),
        last.astype(F32).reshape(1, HERE, BRICK, ENS),
    )


def solution(mesh):
    placed = (
        P("space", None, None),
        P("tm", "space", None, None),
        P("space", None, None),
        P("space", None),
        P(),
        P("space", None, None),
    )
    return jax.shard_map(
        body,
        mesh=mesh,
        in_specs=placed,
        out_specs=(P("tm", "space", None, None), P("tm", "space", None, None)),
        check_vma=False,
    )
```

```python
import functools

import jax
import jax.numpy as jnp
from jax import lax
from jax.experimental import pallas as pl
from jax.experimental.pallas import tpu as pltpu
from jax.sharding import PartitionSpec as P

BRICK = 64
ENS = 128
NB = 6
REACH = 4
Q = 8
STEPS = 4
ITERS = 2
HERE = 8
SLICES = 32
ROWS = HERE * BRICK
HALF = ROWS // 2

MESH = pl.DeviceIdType.MESH
HIGHEST = lax.Precision.HIGHEST
F32 = jnp.float32
BF16 = jnp.bfloat16


def dot(a, b):
    return jnp.dot(a, b, preferred_element_type=F32)


def dot32(a, b):
    return jnp.dot(a, b, preferred_element_type=F32, precision=HIGHEST)


def kernel(
    init_ref, forcing_ref, blocks_ref, neighbours_ref, modes_ref, coarse_ref,
    sol_ref, def_ref,
    fields, weights, home_nbr, nbr, start, state, columns, band, folded, diag, ext00, ext01, ext10, ext11,
    restrict, prolong, coarse_map, strip, toep_high, toep_low, r_buf, in0, in1, err0, err1, got0, got1, all0, all1,
    powers, home_powers, held, home_held, prev_buf, here_buf, home_here, stage,
    field_sem, weight_sem, far_sem, nbr_sem, start_sem, halo_send, halo_recv, swap_send, row_send, row_recv,
    sc_send, sc_recv, all_send, all_recv, power_send, power_recv, forward_send, home_power_sem,
    held_send, home_held_sem, here_send, here_recv, out_send, sol_recv, def_recv,
):
    tm = lax.axis_index("tm")
    sp = lax.axis_index("space")
    c = lax.rem(tm, 2)
    zl = lax.rem(tm // 2, 4)
    x = tm // 8
    y = sp // 2
    zh = lax.rem(sp, 2)
    keeps = c == zh
    moves = c != zh
    j = x * 8 + zl * 2 + zh
    q = 2 * y + c
    partner = (tm - c + zh, sp - zh + c)
    slow, fast = c, 1 - c

    def worker(slice_id):
        return (
            (slice_id // 8) * 8 + lax.rem(slice_id // 2, 4) * 2 + c,
            2 * y + lax.rem(slice_id, 2),
        )

    def in_plane(other):
        return (tm - c + lax.rem(other, 2), (other // 2) * 2 + zh)

    @pl.when(keeps)
    def _():
        pltpu.make_async_copy(blocks_ref, weights, weight_sem).start()
        for i in range(STEPS):
            pltpu.make_async_copy(forcing_ref.at[i], fields.at[i], field_sem.at[i]).start()

    in0[...] = jnp.zeros_like(in0)
    in1[...] = jnp.zeros_like(in1)
    barrier = pltpu.get_barrier_semaphore()

    @pl.when(moves)
    def _():
        @pl.loop(0, HERE)
        def _(other):
            pl.semaphore_signal(
                barrier,
                inc=1,
                device_id=(tm - c + lax.rem(other, 2), (other // 2) * 2 + c),
                device_id_type=MESH,
            )

    @pl.loop(1, HERE)
    def _(d):
        pl.semaphore_signal(
            barrier, inc=1, device_id=in_plane(lax.rem(q + d, HERE)), device_id_type=MESH
        )

    @pl.loop(1, SLICES)
    def _(d):
        pl.semaphore_signal(
            barrier, inc=1, device_id=worker(lax.rem(j + d, SLICES)), device_id_type=MESH
        )

    home_nbr[...] = jnp.zeros_like(home_nbr)
    home_nbr[:, 0:NB] = neighbours_ref[...]
    pl.semaphore_wait(barrier, SLICES - 1 + HERE - 1 + HERE // 2)

    def remote(src, dst, send, recv, device):
        return pltpu.make_async_remote_copy(
            src_ref=src, dst_ref=dst, send_sem=send, recv_sem=recv,
            device_id=device, device_id_type=MESH,
        )

    def arrived(ref, sem):
        pltpu.make_async_copy(ref, ref, sem).wait()

    @pl.when(keeps)
    def _():
        pltpu.make_async_copy(home_nbr, nbr, nbr_sem).start()

    def field(i):
        return remote(
            forcing_ref.at[i], fields.at[i], swap_send.at[i], field_sem.at[i], partner
        )

    fetched = pl.ds(2 * x, 2)
    opposite = pl.ds(2 * lax.rem(x + 2, 4), 2)

    @pl.when(moves)
    def _():
        remote(home_nbr, nbr, swap_send.at[5], nbr_sem, partner).start()
        remote(
            blocks_ref.at[fetched], weights.at[fetched], swap_send.at[4], weight_sem, partner
        ).start()
        arrived(weights.at[pl.ds(0, 2)], swap_send.at[4])
        remote(
            blocks_ref.at[opposite], weights.at[opposite], swap_send.at[7], far_sem, partner
        ).start()

    @pl.when((tm == 0) & (zh == 1))
    def _():
        remote(init_ref, start, swap_send.at[6], start_sem, partner).start()

    @pl.when((tm == 0) & (zh == 0))
    def _():
        pltpu.make_async_copy(init_ref, start, start_sem).start()

    modes = modes_ref[...]
    wide = jnp.concatenate([jnp.concatenate([modes] * 4, axis=1)] * 4, axis=0)
    row = lax.broadcasted_iota(jnp.int32, (4 * Q, HALF), 0)
    col = lax.broadcasted_iota(jnp.int32, (4 * Q, HALF), 1)
    wide = jnp.where(row // Q == col // BRICK, wide, 0.0)
    wide_high = wide.astype(BF16)
    wide_low = (wide - wide_high.astype(F32)).astype(BF16)
    restrict[...] = jnp.concatenate([wide_high, wide_low, wide_high], axis=1)
    prolong[...] = jnp.concatenate(
        [wide_high.astype(F32), wide_low.astype(F32)], axis=0
    ).T.astype(BF16)

    def restricted(values):
        high_part = values.astype(BF16)
        low_part = (values - high_part.astype(F32)).astype(BF16)
        return dot(restrict[...], jnp.concatenate([high_part, high_part, low_part], axis=0))

    def prolonged(rounded):
        return dot(prolong[...], jnp.concatenate([rounded, rounded], axis=0))


    owns = keeps & (zl < 2)
    group = lax.rem(zl, 2)
    @pl.when(owns)
    def _():
        four = coarse_ref[pl.ds(4 * group, 4)].reshape(4 * Q, Q)
        row = lax.broadcasted_iota(jnp.int32, (4 * Q, 4 * Q), 0)
        col = lax.broadcasted_iota(jnp.int32, (4 * Q, 4 * Q), 1)
        power = jnp.where(row // Q == col // Q, jnp.concatenate([four] * 4, axis=1), 0.0)
        chain = (row == col).astype(F32)
        while chain.shape[1] < SLICES * 4 * Q:
            chain = jnp.concatenate([dot32(power, chain), chain], axis=1)
            power = dot32(power, power)
        strip[:, 0 : SLICES * 4 * Q] = chain
        strip[:, SLICES * 4 * Q :] = jnp.zeros((4 * Q, SLICES * 4 * Q), F32)
        near = strip[:, pl.ds(pl.multiple_of((3 - x) * 256, 256), 1280)]
        for d in range(9):
            first = (8 - d) * 4 * Q
            part = near[:, first : first + SLICES * 4 * Q]
            high_part = part.astype(BF16)
            toep_high[d * 4 * Q : (d + 1) * 4 * Q, :] = high_part
            toep_low[d * 4 * Q : (d + 1) * 4 * Q, :] = (part - high_part.astype(F32)).astype(BF16)

    tall = jnp.concatenate([modes] * 16, axis=0).T
    row = lax.broadcasted_iota(jnp.int32, (BRICK, ENS), 0) * 0 + 8 * c
    col = lax.broadcasted_iota(jnp.int32, (BRICK, ENS), 1) // Q
    for b in range(HERE):
        columns[b * BRICK : (b + 1) * BRICK, :] = jnp.where(
            (row + b == col) & (y == x), tall, 0.0
        )

    arrived(nbr, nbr_sem)

    @pl.when(keeps)
    def _():
        arrived(weights, weight_sem)

    @pl.when(moves)
    def _():
        arrived(weights.at[pl.ds(0, 2)], weight_sem)
        for d in (1, 3):
            remote(
                weights.at[fetched], weights.at[fetched], row_send, row_recv,
                (lax.rem(x + d, 4) * 8 + zl * 2 + c, sp),
            ).start()
        field(0).start()
        field(1).start()
        arrived(weights.at[pl.ds(0, 2)], far_sem)
        arrived(weights.at[pl.ds(0, 4)], row_recv)

    brick_ids = lax.broadcasted_iota(jnp.int32, (HERE, 128), 0)
    shift = lax.rem(nbr[...] - (8 * q + brick_ids) + (REACH + 64), 64)
    window = shift + lax.rem(brick_ids, 4)
    nbr[...] = jnp.where(brick_ids < 4, lax.rem(window + 8, 12), window)
    lane_brick = lax.broadcasted_iota(jnp.int32, (BRICK, 128), 1) // BRICK

    @pl.loop(0, HERE)
    def _(b):
        g, b4 = b // 4, lax.rem(b, 4)
        rows = pl.ds(pl.multiple_of(b4 * BRICK, BRICK), BRICK)
        places = nbr[pl.ds(b, 1), :]
        where = [jnp.broadcast_to(places[:, k : k + 1], (BRICK, 128)) for k in range(NB)]
        twice = []
        for k in range(NB + 1):
            block = weights[b, :, k * BRICK : (k + 1) * BRICK].astype(F32)
            twice.append(jnp.concatenate([block, block], axis=1))
        for pair in range(6):
            there = lane_brick + 2 * pair
            block = jnp.zeros((BRICK, 128), F32)
            for k in range(NB):
                block = jnp.where(where[k] == there, twice[k + 1], block)
            band[g, rows, pair * 128 : (pair + 1) * 128] = block.astype(BF16)
        for pair in range(2):
            block = jnp.where(lane_brick + 2 * pair == b4, twice[0], 0.0)
            diag[g, rows, pair * 128 : (pair + 1) * 128] = block.astype(BF16)

    exts = ((ext00, ext01), (ext10, ext11))

    def rows_of(g):
        return pl.ds(pl.multiple_of(g * HALF, HALF), HALF)

    def halo(u, sweep, g):
        ext = exts[u][sweep]
        return remote(
            ext.at[rows_of(g)], ext.at[rows_of(3 - g)],
            halo_send.at[u, sweep, g], halo_recv.at[u, sweep, 1 - g],
            in_plane(lax.rem(q + 7 + 2 * g, HERE)),
        )

    def solved(g, values):
        return dot(diag[g], values.astype(BF16))

    def send_half(u, sweep, g, values):
        exts[u][sweep][rows_of(g), :] = values.astype(BF16)
        halo(u, sweep, g).start()

    def swept(u, sweep, g):
        ext = exts[u][sweep]
        near = dot(band[g, :, : 2 * HALF], ext[0 : 2 * HALF, :])
        inner = solved(g, (state, columns)[u][rows_of(g), :] - near)
        arrived(ext.at[rows_of(2 + g)], halo_recv.at[u, sweep, g])
        return inner - dot(folded[g], ext[rows_of(2 + g), :])

    def halves(g):
        return slice(g * HALF, (g + 1) * HALF)

    def share(i):
        for d in range(1, 4):
            remote(
                powers.at[i, x], powers.at[i, x], power_send.at[i], power_recv.at[i],
                (lax.rem(x + d, 4) * 8 + zl * 2 + c, sp),
            ).start()

    def forward(i):
        arrived(powers.at[i, pl.ds(0, 3)], power_recv.at[i])
        pltpu.make_async_copy(powers.at[i], home_powers.at[i], home_power_sem.at[i]).start()
        remote(
            powers.at[i], home_powers.at[i], forward_send.at[i], home_power_sem.at[i],
            (tm - c + (1 - c), sp),
        ).start()

    def bring(source, target, send, recv):
        @pl.when(keeps)
        def _():
            pltpu.make_async_copy(source, target, recv).start()

        @pl.when(moves)
        def _():
            remote(source, target, send, recv, partner).start()

    @pl.when(j == 0)
    def _():
        arrived(start, start_sem)
        state[...] = start[...]

    @pl.when(j != 0)
    def _():
        state[...] = jnp.zeros_like(state)

    def to_owners(it, incoming):
        @pl.loop(2 * x, 8)
        def _(w):
            g = lax.rem(w, 2)
            owner_tm = (w // 2) * 8 + g * 2 + c
            owner_sp = 2 * y + c
            mine = (owner_tm == tm) & (owner_sp == sp)

            @pl.when(mine)
            def _():
                incoming[j] = r_buf[it, g]

            @pl.when(jnp.logical_not(mine))
            def _():
                remote(
                    r_buf.at[it, g], incoming.at[j], sc_send.at[it, 0], sc_recv.at[it, 0],
                    (owner_tm, owner_sp),
                ).start()

    for u, ref in enumerate((state, columns)):
        for g in (slow, fast):
            send_half(u, 0, g, solved(g, ref[rows_of(g), :]))
    for g in range(2):
        folded[g] = dot(diag[g], band[g, :, 2 * HALF :]).astype(BF16)

    @pl.loop(0, STEPS)
    def _(i):
        @pl.when(moves & (i < 2))
        def _():
            field(i + 2).start()

        for g in (fast, slow):
            for u in range(2):
                send_half(u, 1, g, swept(u, 0, g))
        arrived(fields.at[i], field_sem.at[i])
        for g, u in ((fast, 0), (fast, 1), (slow, 0), (slow, 1)):
            following = swept(u, 1, g)
            arrived(ext00.at[rows_of(0)], halo_send.at[u, 0, g])
            arrived(ext00.at[rows_of(0)], halo_send.at[u, 1, g])
            if u == 0:
                following += fields[i, rows_of(g), :].astype(F32)
                state[rows_of(g), :] = following

                @pl.when(i == STEPS - 1)
                def _():
                    r_buf[0, g] = restricted(following).astype(BF16)
                    if g is slow:
                        to_owners(0, in0)

                held[i, rows_of(g), :] = following.astype(BF16)
            else:
                columns[rows_of(g), :] = following
                powers[i, x, rows_of(g), :] = following.astype(BF16)

            @pl.when(i < STEPS - 1)
            def _():
                send_half(u, 0, g, solved(g, following))

        @pl.when(i < STEPS - 1)
        def _():
            bring(held.at[i], home_held.at[i], held_send.at[i], home_held_sem.at[i])

        @pl.when((i < STEPS - 1) & keeps)
        def _():
            share(i)

        @pl.when((i > 0) & keeps)
        def _():
            forward(i - 1)

    def coarse_part(ref, i, gathered, g):
        matrix = jnp.concatenate([ref[i, n, halves(g), :] for n in range(4)], axis=1)
        return dot(matrix, gathered[...])

    sum_prev = sum_here = None
    for it, (incoming, err, got, gathered) in enumerate(
        ((in0, err0, got0, all0), (in1, err1, got1, all1))
    ):
        if it:
            for g in range(2):
                r_buf[1, g] = (known[g] + dot(coarse_map[g], all0[...])).astype(BF16)
            to_owners(1, in1)
            for g in range(2):
                defect = state[halves(g), :] + coarse_part(powers, STEPS - 1, all0, g)
                stage[STEPS, halves(g), :] = (defect - prolonged(got0[g, 1])).astype(BF16)

        if it:
            bring(stage.at[STEPS], def_ref, out_send, def_recv)
        else:
            share(STEPS - 1)

        @pl.when(owns)
        def _():
            for quarter in range(4):

                @pl.when(x == quarter)
                def _():
                    arrived(incoming.at[pl.ds(0, 8 * quarter + 7)], sc_recv.at[it, 0])

            terms = incoming[...].reshape(SLICES * 4 * Q, ENS)
            errors = dot(toep_high[...], terms) + dot(toep_low[...], terms)
            err[...] = errors.astype(BF16).reshape(9, 4 * Q, ENS)

            @pl.loop(0, 8)
            def _(d):
                there = x * 8 + d

                @pl.when(there == j)
                def _():
                    got[group] = err[pl.ds(d, 2)]

                @pl.when(there != j)
                def _():
                    remote(
                        err.at[pl.ds(d, 2)], got.at[group],
                        sc_send.at[it, 1], sc_recv.at[it, 1], worker(there),
                    ).start()

            arrived(got.at[0], sc_recv.at[it, 1])

        @pl.when(jnp.logical_not(owns))
        def _():
            arrived(got, sc_recv.at[it, 1])

        e_prev = [got[g, 0].astype(F32) for g in range(2)]
        e_here = [got[g, 1].astype(F32) for g in range(2)]
        if it:
            e_prev = [a + b for a, b in zip(e_prev, sum_prev)]
            e_here = [a + b for a, b in zip(e_here, sum_here)]
        sum_prev, sum_here = e_prev, e_here
        mine = pl.ds(pl.multiple_of(q * HERE * Q, HERE * Q), HERE * Q)
        rounded_prev = jnp.concatenate(sum_prev, axis=0).astype(BF16)
        if it == 0:
            gathered[mine, :] = rounded_prev

            @pl.loop(1, HERE)
            def _(d):
                remote(
                    gathered.at[mine], gathered.at[mine], all_send.at[it], all_recv.at[it],
                    in_plane(lax.rem(q + d, HERE)),
                ).start()

            known = [restricted(state[halves(g), :] - prolonged(got[g, 1])) for g in range(2)]
            arrived(powers.at[STEPS - 1, pl.ds(0, 3)], power_recv.at[STEPS - 1])
            for g in range(2):
                last = [powers[STEPS - 1, n, halves(g), :] for n in range(4)]
                last = jnp.concatenate(last, axis=1)
                last = jnp.concatenate([last, last], axis=0)
                coarse_map[g] = dot(restrict[:, : 2 * HALF], last).astype(BF16)
            arrived(gathered.at[pl.ds(0, 7 * HERE * Q)], all_recv.at[it])
        else:
            prev_buf[...] = rounded_prev
            here_buf[...] = jnp.concatenate(sum_here, axis=0).astype(BF16)

            bring(here_buf, home_here, here_send, here_recv)

            @pl.loop(0, HERE)
            def _(d):
                home = lax.rem(sp + d, HERE)
                own = keeps & (home == sp)

                @pl.when(own)
                def _():
                    gathered[mine, :] = prev_buf[...]

                @pl.when(jnp.logical_not(own))
                def _():
                    remote(
                        prev_buf, gathered.at[mine], all_send.at[it], all_recv.at[it],
                        (tm - c + zh, home),
                    ).start()


    for i in range(STEPS - 1):
        arrived(home_held.at[i], home_held_sem.at[i])
        arrived(home_powers.at[i], home_power_sem.at[i])
    arrived(home_here, here_recv)
    for g in range(2):
        part = home_here[g * 4 * Q : (g + 1) * 4 * Q, :]
        stage[STEPS - 1, halves(g), :] = prolonged(part).astype(BF16)
    pltpu.make_async_copy(stage.at[STEPS - 1], sol_ref.at[STEPS - 1], sol_recv).start()

    @pl.when(keeps)
    def _():
        arrived(all1.at[pl.ds(0, 7 * HERE * Q)], all_recv.at[1])

    @pl.when(moves)
    def _():
        arrived(all1, all_recv.at[1])

    for i in range(STEPS - 1):
        for g in range(2):
            value = home_held[i, halves(g), :].astype(F32) + coarse_part(home_powers, i, all1, g)
            stage[i, halves(g), :] = value.astype(BF16)
        pltpu.make_async_copy(stage.at[i], sol_ref.at[i], sol_recv).start()

    for it, incoming in enumerate((in0, in1)):

        @pl.when(owns)
        def _():
            arrived(incoming.at[pl.ds(0, 14)], sc_send.at[it, 1])

        for quarter in range(4):

            @pl.when(owns & (x == quarter))
            def _():
                arrived(incoming.at[pl.ds(0, 7 - 2 * quarter)], sc_send.at[it, 0])

            @pl.when(jnp.logical_not(owns) & (x == quarter))
            def _():
                arrived(incoming.at[pl.ds(0, 8 - 2 * quarter)], sc_send.at[it, 0])

    arrived(all0.at[pl.ds(0, 7 * HERE * Q)], all_send.at[0])
    arrived(powers.at[STEPS - 1, pl.ds(0, 3)], power_send.at[STEPS - 1])

    @pl.when(keeps)
    def _():
        arrived(all0.at[pl.ds(0, 7 * HERE * Q)], all_send.at[1])
        for i in range(STEPS - 1):
            arrived(powers.at[i, pl.ds(0, 3)], power_send.at[i])
            arrived(powers.at[i], forward_send.at[i])

    @pl.when(moves)
    def _():
        arrived(all0, all_send.at[1])
        arrived(home_nbr, swap_send.at[5])
        arrived(weights.at[pl.ds(0, 2)], swap_send.at[7])
        arrived(weights.at[pl.ds(0, 4)], row_send)
        for i in range(STEPS):
            arrived(fields.at[i], swap_send.at[i])
        for i in range(STEPS - 1):
            arrived(held.at[i], held_send.at[i])
        arrived(stage.at[STEPS], out_send)
        arrived(here_buf, here_send)

    @pl.when((tm == 0) & (zh == 1))
    def _():
        arrived(start, swap_send.at[6])

    arrived(sol_ref, sol_recv)
    arrived(def_ref, def_recv)


def body(initial, forcing, brick_blocks, neighbours, coarse_modes, coarse_blocks):
    vmem = pl.BlockSpec(memory_space=pltpu.VMEM)
    hbm = pl.BlockSpec(memory_space=pl.ANY)
    sem = pltpu.SemaphoreType.DMA
    sol, last = pl.pallas_call(
        kernel,
        out_shape=(
            jax.ShapeDtypeStruct((STEPS, ROWS, ENS), BF16),
            jax.ShapeDtypeStruct((ROWS, ENS), BF16),
        ),
        in_specs=[hbm, hbm, hbm, vmem, vmem, vmem],
        out_specs=(hbm, hbm),
        scratch_shapes=[
            pltpu.VMEM((STEPS, ROWS, ENS), BF16),
            pltpu.VMEM((HERE, BRICK, (NB + 1) * BRICK), BF16),
            pltpu.VMEM((HERE, 128), jnp.int32),
            pltpu.VMEM((HERE, 128), jnp.int32),
            pltpu.VMEM((ROWS, ENS), F32),
            pltpu.VMEM((ROWS, ENS), F32),
            pltpu.VMEM((ROWS, ENS), F32),
            pltpu.VMEM((2, HALF, 3 * HALF), BF16),
            pltpu.VMEM((2, HALF, HALF), BF16),
            pltpu.VMEM((2, HALF, HALF), BF16),
            *[pltpu.VMEM((4 * HALF, ENS), BF16)] * 4,
            pltpu.VMEM((4 * Q, 3 * HALF), BF16),
            pltpu.VMEM((HALF, 8 * Q), BF16),
            pltpu.VMEM((2, 4 * Q, HERE * HERE * Q), BF16),
            pltpu.VMEM((4 * Q, 2 * SLICES * 4 * Q), F32),
            pltpu.VMEM((9 * 4 * Q, SLICES * 4 * Q), BF16),
            pltpu.VMEM((9 * 4 * Q, SLICES * 4 * Q), BF16),
            pltpu.VMEM((ITERS, 2, 4 * Q, ENS), BF16),
            *[pltpu.VMEM((SLICES, 4 * Q, ENS), BF16)] * 2,
            *[pltpu.VMEM((9, 4 * Q, ENS), BF16)] * 2,
            *[pltpu.VMEM((2, 2, 4 * Q, ENS), BF16)] * 2,
            *[pltpu.VMEM((HERE * HERE * Q, ENS), BF16)] * 2,
            pltpu.VMEM((STEPS, 4, ROWS, ENS), BF16),
            pltpu.VMEM((STEPS - 1, 4, ROWS, ENS), BF16),
            pltpu.VMEM((STEPS, ROWS, ENS), BF16),
            pltpu.VMEM((STEPS - 1, ROWS, ENS), BF16),
            *[pltpu.VMEM((HERE * Q, ENS), BF16)] * 3,
            pltpu.VMEM((STEPS + 1, ROWS, ENS), BF16),
            sem((STEPS,)),
            sem,
            sem,
            sem,
            sem,
            sem((2, 2, 2)),
            sem((2, 2, 2)),
            sem((8,)),
            sem,
            sem,
            sem((ITERS, 2)),
            sem((ITERS, 2)),
            sem((ITERS,)),
            sem((ITERS,)),
            sem((STEPS,)),
            sem((STEPS,)),
            sem((STEPS - 1,)),
            sem((STEPS - 1,)),
            sem((STEPS - 1,)),
            sem((STEPS - 1,)),
            sem,
            sem,
            sem,
            sem,
            sem,
        ],
        compiler_params=pltpu.CompilerParams(
            collective_id=0, has_side_effects=True, vmem_limit_bytes=60 * 2**20
        ),
    )(
        initial.reshape(ROWS, ENS),
        forcing.reshape(STEPS, ROWS, ENS),
        brick_blocks,
        neighbours,
        coarse_modes,
        coarse_blocks,
    )
    return (
        sol.astype(F32).reshape(STEPS, HERE, BRICK, ENS),
        last.astype(F32).reshape(1, HERE, BRICK, ENS),
    )


def solution(mesh):
    placed = (
        P("space", None, None),
        P("tm", "space", None, None),
        P("space", None, None),
        P("space", None),
        P(),
        P("space", None, None),
    )
    return jax.shard_map(
        body,
        mesh=mesh,
        in_specs=placed,
        out_specs=(P("tm", "space", None, None), P("tm", "space", None, None)),
        check_vma=False,
    )
```

```python
import functools

import jax
import jax.numpy as jnp
from jax import lax
from jax.experimental import pallas as pl
from jax.experimental.pallas import tpu as pltpu
from jax.sharding import PartitionSpec as P

BRICK = 64
ENS = 128
NB = 6
REACH = 4
Q = 8
STEPS = 4
ITERS = 2
HERE = 8
SLICES = 32
ROWS = HERE * BRICK
HALF = ROWS // 2

MESH = pl.DeviceIdType.MESH
HIGHEST = lax.Precision.HIGHEST
F32 = jnp.float32
BF16 = jnp.bfloat16


def dot(a, b):
    return jnp.dot(a, b, preferred_element_type=F32)


def dot32(a, b):
    return jnp.dot(a, b, preferred_element_type=F32, precision=HIGHEST)


def kernel(
    init_ref, forcing_ref, blocks_ref, neighbours_ref, modes_ref, coarse_ref,
    sol_ref, def_ref,
    fields, weights, home_nbr, nbr, start, state, columns, band, folded, diag, ext00, ext01, ext10, ext11,
    restrict, prolong, coarse_map, strip, toep_high, toep_low, r_buf, in0, in1, err0, err1, got0, got1, all0, all1,
    powers, home_powers, held, home_held, prev_buf, here_buf, home_here, stage,
    field_sem, weight_sem, far_sem, nbr_sem, start_sem, halo_send, halo_recv, swap_send, row_send, row_recv,
    sc_send, sc_recv, all_send, all_recv, power_send, power_recv, forward_send, home_power_sem,
    held_send, home_held_sem, here_send, here_recv, out_send, sol_recv, def_recv,
):
    tm = lax.axis_index("tm")
    sp = lax.axis_index("space")
    c = lax.rem(tm, 2)
    zl = lax.rem(tm // 2, 4)
    x = tm // 8
    y = sp // 2
    zh = lax.rem(sp, 2)
    keeps = c == zh
    moves = c != zh
    j = x * 8 + zl * 2 + zh
    q = 2 * y + c
    partner = (tm - c + zh, sp - zh + c)
    slow, fast = c, 1 - c

    def worker(slice_id):
        return (
            (slice_id // 8) * 8 + lax.rem(slice_id // 2, 4) * 2 + c,
            2 * y + lax.rem(slice_id, 2),
        )

    def in_plane(other):
        return (tm - c + lax.rem(other, 2), (other // 2) * 2 + zh)

    @pl.when(keeps)
    def _():
        pltpu.make_async_copy(blocks_ref, weights, weight_sem).start()
        for i in range(STEPS):
            pltpu.make_async_copy(forcing_ref.at[i], fields.at[i], field_sem.at[i]).start()

    in0[...] = jnp.zeros_like(in0)
    in1[...] = jnp.zeros_like(in1)
    barrier = pltpu.get_barrier_semaphore()

    @pl.when(moves)
    def _():
        @pl.loop(0, HERE)
        def _(other):
            pl.semaphore_signal(
                barrier,
                inc=1,
                device_id=(tm - c + lax.rem(other, 2), (other // 2) * 2 + c),
                device_id_type=MESH,
            )

    @pl.loop(1, HERE)
    def _(d):
        pl.semaphore_signal(
            barrier, inc=1, device_id=in_plane(lax.rem(q + d, HERE)), device_id_type=MESH
        )

    @pl.loop(1, SLICES)
    def _(d):
        pl.semaphore_signal(
            barrier, inc=1, device_id=worker(lax.rem(j + d, SLICES)), device_id_type=MESH
        )

    home_nbr[...] = jnp.zeros_like(home_nbr)
    home_nbr[:, 0:NB] = neighbours_ref[...]
    pl.semaphore_wait(barrier, SLICES - 1 + HERE - 1 + HERE // 2)

    def remote(src, dst, send, recv, device):
        return pltpu.make_async_remote_copy(
            src_ref=src, dst_ref=dst, send_sem=send, recv_sem=recv,
            device_id=device, device_id_type=MESH,
        )

    def arrived(ref, sem):
        pltpu.make_async_copy(ref, ref, sem).wait()

    @pl.when(keeps)
    def _():
        pltpu.make_async_copy(home_nbr, nbr, nbr_sem).start()

    def field(i):
        return remote(
            forcing_ref.at[i], fields.at[i], swap_send.at[i], field_sem.at[i], partner
        )

    fetched = pl.ds(2 * x, 2)
    opposite = pl.ds(2 * lax.rem(x + 2, 4), 2)

    @pl.when(moves)
    def _():
        remote(home_nbr, nbr, swap_send.at[5], nbr_sem, partner).start()
        remote(
            blocks_ref.at[fetched], weights.at[fetched], swap_send.at[4], weight_sem, partner
        ).start()
        arrived(weights.at[pl.ds(0, 2)], swap_send.at[4])
        remote(
            blocks_ref.at[opposite], weights.at[opposite], swap_send.at[7], far_sem, partner
        ).start()

    @pl.when((tm == 0) & (zh == 1))
    def _():
        remote(init_ref, start, swap_send.at[6], start_sem, partner).start()

    @pl.when((tm == 0) & (zh == 0))
    def _():
        pltpu.make_async_copy(init_ref, start, start_sem).start()

    modes = modes_ref[...]
    wide = jnp.concatenate([jnp.concatenate([modes] * 4, axis=1)] * 4, axis=0)
    row = lax.broadcasted_iota(jnp.int32, (4 * Q, HALF), 0)
    col = lax.broadcasted_iota(jnp.int32, (4 * Q, HALF), 1)
    wide = jnp.where(row // Q == col // BRICK, wide, 0.0)
    wide_high = wide.astype(BF16)
    wide_low = (wide - wide_high.astype(F32)).astype(BF16)
    restrict[...] = jnp.concatenate([wide_high, wide_low, wide_high], axis=1)
    prolong[...] = jnp.concatenate(
        [wide_high.astype(F32), wide_low.astype(F32)], axis=0
    ).T.astype(BF16)

    def restricted(values):
        high_part = values.astype(BF16)
        low_part = (values - high_part.astype(F32)).astype(BF16)
        return dot(restrict[...], jnp.concatenate([high_part, high_part, low_part], axis=0))

    def prolonged(rounded):
        return dot(prolong[...], jnp.concatenate([rounded, rounded], axis=0))


    owns = keeps & (zl < 2)
    group = lax.rem(zl, 2)
    @pl.when(owns)
    def _():
        four = coarse_ref[pl.ds(4 * group, 4)].reshape(4 * Q, Q)
        row = lax.broadcasted_iota(jnp.int32, (4 * Q, 4 * Q), 0)
        col = lax.broadcasted_iota(jnp.int32, (4 * Q, 4 * Q), 1)
        power = jnp.where(row // Q == col // Q, jnp.concatenate([four] * 4, axis=1), 0.0)
        chain = (row == col).astype(F32)
        while chain.shape[1] < SLICES * 4 * Q:
            chain = jnp.concatenate([dot32(power, chain), chain], axis=1)
            power = dot32(power, power)
        strip[:, 0 : SLICES * 4 * Q] = chain
        strip[:, SLICES * 4 * Q :] = jnp.zeros((4 * Q, SLICES * 4 * Q), F32)
        near = strip[:, pl.ds(pl.multiple_of((3 - x) * 256, 256), 1280)]
        for d in range(9):
            first = (8 - d) * 4 * Q
            part = near[:, first : first + SLICES * 4 * Q]
            high_part = part.astype(BF16)
            toep_high[d * 4 * Q : (d + 1) * 4 * Q, :] = high_part
            toep_low[d * 4 * Q : (d + 1) * 4 * Q, :] = (part - high_part.astype(F32)).astype(BF16)

    tall = jnp.concatenate([modes] * 16, axis=0).T
    row = lax.broadcasted_iota(jnp.int32, (BRICK, ENS), 0) * 0 + 8 * c
    col = lax.broadcasted_iota(jnp.int32, (BRICK, ENS), 1) // Q
    for b in range(HERE):
        columns[b * BRICK : (b + 1) * BRICK, :] = jnp.where(
            (row + b == col) & (y == x), tall, 0.0
        )

    arrived(nbr, nbr_sem)

    @pl.when(keeps)
    def _():
        arrived(weights, weight_sem)

    @pl.when(moves)
    def _():
        arrived(weights.at[pl.ds(0, 2)], weight_sem)
        for d in (1, 3):
            remote(
                weights.at[fetched], weights.at[fetched], row_send, row_recv,
                (lax.rem(x + d, 4) * 8 + zl * 2 + c, sp),
            ).start()
        field(0).start()
        field(1).start()
        arrived(weights.at[pl.ds(0, 2)], far_sem)
        arrived(weights.at[pl.ds(0, 4)], row_recv)

    brick_ids = lax.broadcasted_iota(jnp.int32, (HERE, 128), 0)
    shift = lax.rem(nbr[...] - (8 * q + brick_ids) + (REACH + 64), 64)
    window = shift + lax.rem(brick_ids, 4)
    nbr[...] = jnp.where(brick_ids < 4, lax.rem(window + 8, 12), window)
    lane_brick = lax.broadcasted_iota(jnp.int32, (BRICK, 128), 1) // BRICK

    @pl.loop(0, HERE)
    def _(b):
        g, b4 = b // 4, lax.rem(b, 4)
        rows = pl.ds(pl.multiple_of(b4 * BRICK, BRICK), BRICK)
        places = nbr[pl.ds(b, 1), :]
        where = [jnp.broadcast_to(places[:, k : k + 1], (BRICK, 128)) for k in range(NB)]
        twice = []
        for k in range(NB + 1):
            block = weights[b, :, k * BRICK : (k + 1) * BRICK].astype(F32)
            twice.append(jnp.concatenate([block, block], axis=1))
        for pair in range(6):
            there = lane_brick + 2 * pair
            block = jnp.zeros((BRICK, 128), F32)
            for k in range(NB):
                block = jnp.where(where[k] == there, twice[k + 1], block)
            band[g, rows, pair * 128 : (pair + 1) * 128] = block.astype(BF16)
        for pair in range(2):
            block = jnp.where(lane_brick + 2 * pair == b4, twice[0], 0.0)
            diag[g, rows, pair * 128 : (pair + 1) * 128] = block.astype(BF16)

    exts = ((ext00, ext01), (ext10, ext11))

    def rows_of(g):
        return pl.ds(pl.multiple_of(g * HALF, HALF), HALF)

    def halo(u, sweep, g):
        ext = exts[u][sweep]
        return remote(
            ext.at[rows_of(g)], ext.at[rows_of(3 - g)],
            halo_send.at[u, sweep, g], halo_recv.at[u, sweep, 1 - g],
            in_plane(lax.rem(q + 7 + 2 * g, HERE)),
        )

    def solved(g, values):
        return dot(diag[g], values.astype(BF16))

    def send_half(u, sweep, g, values):
        exts[u][sweep][rows_of(g), :] = values.astype(BF16)
        halo(u, sweep, g).start()

    def swept(u, sweep, g):
        ext = exts[u][sweep]
        near = dot(band[g, :, : 2 * HALF], ext[0 : 2 * HALF, :])
        inner = solved(g, (state, columns)[u][rows_of(g), :] - near)
        arrived(ext.at[rows_of(2 + g)], halo_recv.at[u, sweep, g])
        return inner - dot(folded[g], ext[rows_of(2 + g), :])

    def halves(g):
        return slice(g * HALF, (g + 1) * HALF)

    def share(i):
        for d in range(1, 4):
            remote(
                powers.at[i, x], powers.at[i, x], power_send.at[i], power_recv.at[i],
                (lax.rem(x + d, 4) * 8 + zl * 2 + c, sp),
            ).start()

    def forward(i):
        arrived(powers.at[i, pl.ds(0, 3)], power_recv.at[i])
        pltpu.make_async_copy(powers.at[i], home_powers.at[i], home_power_sem.at[i]).start()
        remote(
            powers.at[i], home_powers.at[i], forward_send.at[i], home_power_sem.at[i],
            (tm - c + (1 - c), sp),
        ).start()

    def bring(source, target, send, recv):
        @pl.when(keeps)
        def _():
            pltpu.make_async_copy(source, target, recv).start()

        @pl.when(moves)
        def _():
            remote(source, target, send, recv, partner).start()

    @pl.when(j == 0)
    def _():
        arrived(start, start_sem)
        state[...] = start[...]

    @pl.when(j != 0)
    def _():
        state[...] = jnp.zeros_like(state)

    def to_owners(it, incoming):
        @pl.loop(2 * x, 8)
        def _(w):
            g = lax.rem(w, 2)
            owner_tm = (w // 2) * 8 + g * 2 + c
            owner_sp = 2 * y + c
            mine = (owner_tm == tm) & (owner_sp == sp)

            @pl.when(mine)
            def _():
                incoming[j] = r_buf[it, g]

            @pl.when(jnp.logical_not(mine))
            def _():
                remote(
                    r_buf.at[it, g], incoming.at[j], sc_send.at[it, 0], sc_recv.at[it, 0],
                    (owner_tm, owner_sp),
                ).start()

    for u, ref in enumerate((state, columns)):
        for g in (slow, fast):
            send_half(u, 0, g, solved(g, ref[rows_of(g), :]))
    for g in range(2):
        folded[g] = dot(diag[g], band[g, :, 2 * HALF :]).astype(BF16)

    @pl.loop(0, STEPS)
    def _(i):
        @pl.when(moves & (i < 2))
        def _():
            field(i + 2).start()

        for g in (fast, slow):
            for u in range(2):
                send_half(u, 1, g, swept(u, 0, g))
        arrived(fields.at[i], field_sem.at[i])
        for g, u in ((fast, 0), (fast, 1), (slow, 0), (slow, 1)):
            following = swept(u, 1, g)
            arrived(ext00.at[rows_of(0)], halo_send.at[u, 0, g])
            arrived(ext00.at[rows_of(0)], halo_send.at[u, 1, g])
            if u == 0:
                following += fields[i, rows_of(g), :].astype(F32)
                state[rows_of(g), :] = following

                @pl.when(i == STEPS - 1)
                def _():
                    r_buf[0, g] = restricted(following).astype(BF16)
                    if g is slow:
                        to_owners(0, in0)

                held[i, rows_of(g), :] = following.astype(BF16)
            else:
                columns[rows_of(g), :] = following
                powers[i, x, rows_of(g), :] = following.astype(BF16)

            @pl.when(i < STEPS - 1)
            def _():
                send_half(u, 0, g, solved(g, following))

        @pl.when(i < STEPS - 1)
        def _():
            bring(held.at[i], home_held.at[i], held_send.at[i], home_held_sem.at[i])

        @pl.when((i < STEPS - 1) & keeps)
        def _():
            share(i)

        @pl.when((i > 0) & keeps)
        def _():
            forward(i - 1)

    def coarse_part(ref, i, gathered, g):
        matrix = jnp.concatenate([ref[i, n, halves(g), :] for n in range(4)], axis=1)
        return dot(matrix, gathered[...])

    sum_prev = sum_here = None
    for it, (incoming, err, got, gathered) in enumerate(
        ((in0, err0, got0, all0), (in1, err1, got1, all1))
    ):
        if it:
            for g in range(2):
                r_buf[1, g] = (known[g] + dot(coarse_map[g], all0[...])).astype(BF16)
            to_owners(1, in1)
            for g in range(2):
                defect = state[halves(g), :] + coarse_part(powers, STEPS - 1, all0, g)
                stage[STEPS, halves(g), :] = (defect - prolonged(got0[g, 1])).astype(BF16)

        if it:
            bring(stage.at[STEPS], def_ref, out_send, def_recv)
        else:
            share(STEPS - 1)

        @pl.when(owns)
        def _():
            for quarter in range(4):

                @pl.when(x == quarter)
                def _():
                    arrived(incoming.at[pl.ds(0, 8 * quarter + 7)], sc_recv.at[it, 0])

            terms = incoming[...].reshape(SLICES * 4 * Q, ENS)
            errors = dot(toep_high[...], terms) + dot(toep_low[...], terms)
            err[...] = errors.astype(BF16).reshape(9, 4 * Q, ENS)

            @pl.loop(0, 8, unroll=True)
            def _(d):
                there = x * 8 + d

                @pl.when(there == j)
                def _():
                    got[group] = err[pl.ds(d, 2)]

                @pl.when(there != j)
                def _():
                    remote(
                        err.at[pl.ds(d, 2)], got.at[group],
                        sc_send.at[it, 1], sc_recv.at[it, 1], worker(there),
                    ).start()

            arrived(got.at[0], sc_recv.at[it, 1])

        @pl.when(jnp.logical_not(owns))
        def _():
            arrived(got, sc_recv.at[it, 1])

        e_prev = [got[g, 0].astype(F32) for g in range(2)]
        e_here = [got[g, 1].astype(F32) for g in range(2)]
        if it:
            e_prev = [a + b for a, b in zip(e_prev, sum_prev)]
            e_here = [a + b for a, b in zip(e_here, sum_here)]
        sum_prev, sum_here = e_prev, e_here
        mine = pl.ds(pl.multiple_of(q * HERE * Q, HERE * Q), HERE * Q)
        rounded_prev = jnp.concatenate(sum_prev, axis=0).astype(BF16)
        if it == 0:
            gathered[mine, :] = rounded_prev

            @pl.loop(1, HERE, unroll=True)
            def _(d):
                remote(
                    gathered.at[mine], gathered.at[mine], all_send.at[it], all_recv.at[it],
                    in_plane(lax.rem(q + d, HERE)),
                ).start()

            known = [restricted(state[halves(g), :] - prolonged(got[g, 1])) for g in range(2)]
            arrived(powers.at[STEPS - 1, pl.ds(0, 3)], power_recv.at[STEPS - 1])
            for g in range(2):
                last = [powers[STEPS - 1, n, halves(g), :] for n in range(4)]
                last = jnp.concatenate(last, axis=1)
                last = jnp.concatenate([last, last], axis=0)
                coarse_map[g] = dot(restrict[:, : 2 * HALF], last).astype(BF16)
            arrived(gathered.at[pl.ds(0, 7 * HERE * Q)], all_recv.at[it])
        else:
            prev_buf[...] = rounded_prev
            here_buf[...] = jnp.concatenate(sum_here, axis=0).astype(BF16)

            bring(here_buf, home_here, here_send, here_recv)

            @pl.loop(0, HERE, unroll=True)
            def _(d):
                home = lax.rem(sp + d, HERE)
                own = keeps & (home == sp)

                @pl.when(own)
                def _():
                    gathered[mine, :] = prev_buf[...]

                @pl.when(jnp.logical_not(own))
                def _():
                    remote(
                        prev_buf, gathered.at[mine], all_send.at[it], all_recv.at[it],
                        (tm - c + zh, home),
                    ).start()


    for i in range(STEPS - 1):
        arrived(home_held.at[i], home_held_sem.at[i])
        arrived(home_powers.at[i], home_power_sem.at[i])
    arrived(home_here, here_recv)
    for g in range(2):
        part = home_here[g * 4 * Q : (g + 1) * 4 * Q, :]
        stage[STEPS - 1, halves(g), :] = prolonged(part).astype(BF16)
    pltpu.make_async_copy(stage.at[STEPS - 1], sol_ref.at[STEPS - 1], sol_recv).start()

    @pl.when(keeps)
    def _():
        arrived(all1.at[pl.ds(0, 7 * HERE * Q)], all_recv.at[1])

    @pl.when(moves)
    def _():
        arrived(all1, all_recv.at[1])

    for i in range(STEPS - 1):
        for g in range(2):
            value = home_held[i, halves(g), :].astype(F32) + coarse_part(home_powers, i, all1, g)
            stage[i, halves(g), :] = value.astype(BF16)
        pltpu.make_async_copy(stage.at[i], sol_ref.at[i], sol_recv).start()

    for it, incoming in enumerate((in0, in1)):

        @pl.when(owns)
        def _():
            arrived(incoming.at[pl.ds(0, 14)], sc_send.at[it, 1])

        for quarter in range(4):

            @pl.when(owns & (x == quarter))
            def _():
                arrived(incoming.at[pl.ds(0, 7 - 2 * quarter)], sc_send.at[it, 0])

            @pl.when(jnp.logical_not(owns) & (x == quarter))
            def _():
                arrived(incoming.at[pl.ds(0, 8 - 2 * quarter)], sc_send.at[it, 0])

    arrived(all0.at[pl.ds(0, 7 * HERE * Q)], all_send.at[0])
    arrived(powers.at[STEPS - 1, pl.ds(0, 3)], power_send.at[STEPS - 1])

    @pl.when(keeps)
    def _():
        arrived(all0.at[pl.ds(0, 7 * HERE * Q)], all_send.at[1])
        for i in range(STEPS - 1):
            arrived(powers.at[i, pl.ds(0, 3)], power_send.at[i])
            arrived(powers.at[i], forward_send.at[i])

    @pl.when(moves)
    def _():
        arrived(all0, all_send.at[1])
        arrived(home_nbr, swap_send.at[5])
        arrived(weights.at[pl.ds(0, 2)], swap_send.at[7])
        arrived(weights.at[pl.ds(0, 4)], row_send)
        for i in range(STEPS):
            arrived(fields.at[i], swap_send.at[i])
        for i in range(STEPS - 1):
            arrived(held.at[i], held_send.at[i])
        arrived(stage.at[STEPS], out_send)
        arrived(here_buf, here_send)

    @pl.when((tm == 0) & (zh == 1))
    def _():
        arrived(start, swap_send.at[6])

    arrived(sol_ref, sol_recv)
    arrived(def_ref, def_recv)


def body(initial, forcing, brick_blocks, neighbours, coarse_modes, coarse_blocks):
    vmem = pl.BlockSpec(memory_space=pltpu.VMEM)
    hbm = pl.BlockSpec(memory_space=pl.ANY)
    sem = pltpu.SemaphoreType.DMA
    sol, last = pl.pallas_call(
        kernel,
        out_shape=(
            jax.ShapeDtypeStruct((STEPS, ROWS, ENS), BF16),
            jax.ShapeDtypeStruct((ROWS, ENS), BF16),
        ),
        in_specs=[hbm, hbm, hbm, vmem, vmem, vmem],
        out_specs=(hbm, hbm),
        scratch_shapes=[
            pltpu.VMEM((STEPS, ROWS, ENS), BF16),
            pltpu.VMEM((HERE, BRICK, (NB + 1) * BRICK), BF16),
            pltpu.VMEM((HERE, 128), jnp.int32),
            pltpu.VMEM((HERE, 128), jnp.int32),
            pltpu.VMEM((ROWS, ENS), F32),
            pltpu.VMEM((ROWS, ENS), F32),
            pltpu.VMEM((ROWS, ENS), F32),
            pltpu.VMEM((2, HALF, 3 * HALF), BF16),
            pltpu.VMEM((2, HALF, HALF), BF16),
            pltpu.VMEM((2, HALF, HALF), BF16),
            *[pltpu.VMEM((4 * HALF, ENS), BF16)] * 4,
            pltpu.VMEM((4 * Q, 3 * HALF), BF16),
            pltpu.VMEM((HALF, 8 * Q), BF16),
            pltpu.VMEM((2, 4 * Q, HERE * HERE * Q), BF16),
            pltpu.VMEM((4 * Q, 2 * SLICES * 4 * Q), F32),
            pltpu.VMEM((9 * 4 * Q, SLICES * 4 * Q), BF16),
            pltpu.VMEM((9 * 4 * Q, SLICES * 4 * Q), BF16),
            pltpu.VMEM((ITERS, 2, 4 * Q, ENS), BF16),
            *[pltpu.VMEM((SLICES, 4 * Q, ENS), BF16)] * 2,
            *[pltpu.VMEM((9, 4 * Q, ENS), BF16)] * 2,
            *[pltpu.VMEM((2, 2, 4 * Q, ENS), BF16)] * 2,
            *[pltpu.VMEM((HERE * HERE * Q, ENS), BF16)] * 2,
            pltpu.VMEM((STEPS, 4, ROWS, ENS), BF16),
            pltpu.VMEM((STEPS - 1, 4, ROWS, ENS), BF16),
            pltpu.VMEM((STEPS, ROWS, ENS), BF16),
            pltpu.VMEM((STEPS - 1, ROWS, ENS), BF16),
            *[pltpu.VMEM((HERE * Q, ENS), BF16)] * 3,
            pltpu.VMEM((STEPS + 1, ROWS, ENS), BF16),
            sem((STEPS,)),
            sem,
            sem,
            sem,
            sem,
            sem((2, 2, 2)),
            sem((2, 2, 2)),
            sem((8,)),
            sem,
            sem,
            sem((ITERS, 2)),
            sem((ITERS, 2)),
            sem((ITERS,)),
            sem((ITERS,)),
            sem((STEPS,)),
            sem((STEPS,)),
            sem((STEPS - 1,)),
            sem((STEPS - 1,)),
            sem((STEPS - 1,)),
            sem((STEPS - 1,)),
            sem,
            sem,
            sem,
            sem,
            sem,
        ],
        compiler_params=pltpu.CompilerParams(
            collective_id=0, has_side_effects=True, vmem_limit_bytes=60 * 2**20
        ),
    )(
        initial.reshape(ROWS, ENS),
        forcing.reshape(STEPS, ROWS, ENS),
        brick_blocks,
        neighbours,
        coarse_modes,
        coarse_blocks,
    )
    return (
        sol.astype(F32).reshape(STEPS, HERE, BRICK, ENS),
        last.astype(F32).reshape(1, HERE, BRICK, ENS),
    )


def solution(mesh):
    placed = (
        P("space", None, None),
        P("tm", "space", None, None),
        P("space", None, None),
        P("space", None),
        P(),
        P("space", None, None),
    )
    return jax.shard_map(
        body,
        mesh=mesh,
        in_specs=placed,
        out_specs=(P("tm", "space", None, None), P("tm", "space", None, None)),
        check_vma=False,
    )
```
